256 devices in a mesh: azim: 64 (over z, x_hi, y), span: 4 (over x_lo, core).
Axes of the slice: x: 4 (x_hi: 2, x_lo: 2; x = x_hi * 2 + x_lo), y: 4, z: 8, core: 2. Of those that a mesh axis runs over, the one named last changes fastest.
Arguments:
- field: float32 [2, 8, 64, 8192], P(None, None, 'span', 'azim'), may hold values from -6 to 6
- positions: float32 [3, 64, 8192], P(None, 'span', 'azim'), may hold values from -1366 to 1366, as said below
- normals: float32 [3, 64, 8192], P(None, 'span', 'azim'), may hold values from -2 to 2, as said below
- areas: float32 [64, 8192], P('span', 'azim'), may hold values from 0.5 to 2
- col_cluster: int32 [64, 4, 64, 2], P('azim', 'span'), may hold values from 0 to 15
- block_count: int32 [64, 4, 64], P('azim', 'span'), may hold values from 0 to 2, as said below
- row_cluster: int32 [64, 4, 64, 2], P('azim', 'span'), may hold values from 0 to 63
- v_factors: float32 [64, 4, 64, 2, 2, 24, 128], P('azim', 'span'), may hold values from -0.5 to 0.5
- u_factors: float32 [64, 4, 64, 2, 2, 24, 128], P('azim', 'span'), may hold values from -0.4375 to 0.4375
Outputs:
- result: float32 [2, 8, 64, 8192], P(None, None, 'span', 'azim')
The draws below stay inside these ranges and needn't reach their ends.
Inputs may be any that keep to these rules, and one draw needn't show every extreme that they name: `positions`: angles follow the azimuth column and heights the axial row, so that distinct panels lie 0.5 or more apart. `normals`: tangential and axial components lie within half of the radial one. `block_count`: slot k of a sender and receiving sector holds a block when k < the count; the count of a sector with itself is 0, and every sender fills all 2 slots to some sector.
All inputs are finite; a program needn't handle non-finite values.
Results may differ from the reference program's by a relative error of at most 0.0003.
Values sent between devices are 32-bit elements; how exact they have to be, the bound alone decides.
No kernel may reach another device: no remote copies, remote signals or barrier semaphores. Data moves between devices by JAX's collectives and lax.ppermute only.
A program may use at most 64 MiB of HBM per device.

```python
import math
import jax
import jax.numpy as jnp
from jax import lax

PSP = 16
PAZ = 128
RANK = 24
NRHS = 8
CAP = 2
NSP = 64
NAZ = 8192
N_AZIM = 64
N_SPAN = 4


def panel_angles(key):
    shared = jax.random.fold_in(key, 101)
    jitter = jax.random.uniform(shared, (NSP, NAZ), jnp.float32, -0.2, 0.2)
    column = jnp.arange(NAZ, dtype=jnp.float32)[None, :]
    return (column + jitter) * (2.0 * math.pi / NAZ)


def draw_positions(key, part):
    angle_grid = panel_angles(key)
    key = jax.random.fold_in(key, 1)
    key_radius, key_height = jax.random.split(key)
    radius = NAZ / (2.0 * math.pi) + jax.random.uniform(key_radius, (NSP, NAZ), jnp.float32, -0.3, 0.3)
    height = jnp.arange(NSP, dtype=jnp.float32)[:, None] + jax.random.uniform(key_height, (NSP, NAZ), jnp.float32, -0.2, 0.2)
    return jnp.stack([radius * jnp.cos(angle_grid), radius * jnp.sin(angle_grid), height], 0)


def draw_normals(key, part):
    angle_grid = panel_angles(key)
    key = jax.random.fold_in(key, 2)
    key_tilt, key_axial = jax.random.split(key)
    tilt = jax.random.uniform(key_tilt, (NSP, NAZ), jnp.float32, -0.5, 0.5)
    axial = jax.random.uniform(key_axial, (NSP, NAZ), jnp.float32, -0.5, 0.5)
    cosine = jnp.cos(angle_grid)
    sine = jnp.sin(angle_grid)
    return jnp.stack([cosine - tilt * sine, sine + tilt * cosine, axial], 0)


def draw_block_count(key, part):
    key = jax.random.fold_in(key, 3)
    key_base, key_heavy = jax.random.split(key)
    base_count = jax.random.randint(key_base, (N_AZIM, N_SPAN, N_AZIM), 0, CAP + 1)
    heavy_sector = jax.random.randint(key_heavy, (1, 1, N_AZIM), 0, 2)
    counts = jnp.minimum(base_count + heavy_sector * CAP, CAP)
    sender = jnp.arange(N_AZIM, dtype=jnp.int32)[:, None, None]
    target_sector = jnp.arange(N_AZIM, dtype=jnp.int32)[None, None, :]
    counts = jnp.where(target_sector == (sender + N_AZIM // 2) % N_AZIM, CAP, counts)
    counts = jnp.where(target_sector == sender, 0, counts)
    return counts.astype(jnp.int32)


def place_ends(entries, own_key, least, high):
    dims = entries.shape
    spot = [jax.random.randint(jax.random.fold_in(own_key, axis), (), 0, dims[axis]) for axis in range(len(dims))]
    entries = entries.at[tuple(spot)].set(least)
    longest = dims.index(max(dims))
    spot[longest] = (spot[longest] + 1) % dims[longest]
    return entries.at[tuple(spot)].set(high)


def block_scale(stream_key, shape, cuts, smallest, top_value):
    level, own = 1.0, jax.random.fold_in(stream_key, 6)
    for dim, blocks in cuts:
        heights = jnp.exp(jax.random.uniform(jax.random.fold_in(own, dim), (blocks,), jnp.float32, smallest / len(cuts), top_value / len(cuts)))
        level = level * jnp.repeat(heights, shape[dim] // blocks).reshape([-1 if axis == dim else 1 for axis in range(len(shape))])
    return level


def bell_draw(stream_key, extent, width, most, cuts=(), kind=jnp.bfloat16):
    factor_of = block_scale(stream_key, extent, cuts, -0.22, 0.18) if cuts else 1.0
    values = jax.random.normal(stream_key, extent, jnp.float32) * width * factor_of
    return jnp.minimum(jnp.maximum(values, -most), most).astype(kind)


def setup_inputs(seed: int = 0) -> dict:
    splits = jax.random.split(jax.random.key(seed), 10)
    return {
        "field": bell_draw(splits[0], (2, NRHS, NSP, NAZ), 1.0, 6.0, ((2, 4), (3, 64)), jnp.float32),
        "positions": draw_positions(jax.random.fold_in(splits[9], 71), 0),
        "normals": draw_normals(jax.random.fold_in(splits[9], 71), 0),
        "areas": jnp.clip(jnp.exp(math.log(2.0) - 1.3862944 * jax.random.uniform(splits[3], (NSP, NAZ), jnp.float32) ** block_scale(splits[3], (NSP, NAZ), ((0, 4), (1, 64)), -0.2, 0.2)), 0.5, 2.0),
        "col_cluster": place_ends(jax.random.randint(splits[4], (N_AZIM, N_SPAN, N_AZIM, CAP), 0, PSP), jax.random.fold_in(splits[4], 1), 0, PSP - 1).astype(jnp.int32),
        "block_count": draw_block_count(jax.random.fold_in(splits[9], 71), 0),
        "row_cluster": place_ends(jax.random.randint(splits[6], (N_AZIM, N_SPAN, N_AZIM, CAP), 0, NSP), jax.random.fold_in(splits[6], 1), 0, NSP - 1).astype(jnp.int32),
        "v_factors": bell_draw(splits[7], (N_AZIM, N_SPAN, N_AZIM, CAP, 2, RANK, PAZ), PAZ ** -0.5, 0.5, ((0, 64), (1, 4)), jnp.float32),
        "u_factors": bell_draw(splits[8], (N_AZIM, N_SPAN, N_AZIM, CAP, 2, RANK, PAZ), (RANK * 8) ** -0.5, 0.4375, ((0, 64), (1, 4)), jnp.float32),
    }


wavenumber = 0.9
coupling = 1.1
highest = lax.Precision.HIGHEST

def pair_kernel(delta, normal, area, self_pair, nearby):
    squared = delta[0] * delta[0] + delta[1] * delta[1] + delta[2] * delta[2]
    distance = jnp.sqrt(jnp.where(self_pair, 1.0, squared))
    slant = (delta[0] * normal[0] + delta[1] * normal[1] + delta[2] * normal[2]) / distance
    green = jnp.where(nearby, area / (4.0 * math.pi * distance), 0.0)
    first = slant / distance
    second = wavenumber * slant + coupling
    cosine = jnp.cos(wavenumber * distance)
    sine = jnp.sin(wavenumber * distance)
    return (green * (cosine * first + sine * second), green * (sine * first - cosine * second))

def near_field(field, positions, normals, areas):
    reach = PAZ // 4
    same_row = jnp.eye(PSP, dtype=bool)[:, :, None]
    strips = []
    for strip_index in range(N_SPAN):
        low = strip_index * PSP
        strip_field = field[:, :, low:low + PSP]
        strip_pos = positions[:, low:low + PSP]
        strip_normal = normals[:, low:low + PSP]
        strip_area = areas[low:low + PSP]

        def step(turn, accum):
            offset = turn - reach
            src_pos = jnp.roll(strip_pos, offset, axis=2)
            src_normal = jnp.roll(strip_normal, offset, axis=2)
            src_area = jnp.roll(strip_area, offset, axis=1)
            src_field = jnp.roll(strip_field, offset, axis=3)
            delta = strip_pos[:, :, None] - src_pos[:, None]
            self_pair = same_row & (offset == 0)
            nearby = jnp.logical_not(self_pair)
            kern_re, kern_im = pair_kernel(delta, src_normal[:, None], src_area[None], self_pair, nearby)
            prod_re = jnp.einsum('tsn,cusn->cutn', kern_re, src_field, precision=highest)
            prod_im = jnp.einsum('tsn,cusn->cutn', kern_im, src_field, precision=highest)
            return accum + jnp.stack([prod_re[0] - prod_im[1], prod_re[1] + prod_im[0]], 0)
        strips.append(lax.fori_loop(0, 2 * reach + 1, step, jnp.zeros(strip_field.shape, jnp.float32)))
    return jnp.concatenate(strips, axis=2)

def far_field(field, col_cluster, block_count, row_cluster, v_factors, u_factors):
    blocks = field.reshape(2, NRHS, NSP, N_AZIM, PAZ)
    slot_ids = jnp.arange(CAP, dtype=jnp.int32)

    def sender(sector):
        local = lax.dynamic_index_in_dim(blocks, sector, 3, keepdims=False)
        row_ids = (jnp.arange(N_SPAN, dtype=jnp.int32)[:, None, None] * PSP + col_cluster[sector]).astype(jnp.int32)
        picked = jnp.take(local, row_ids, axis=2)
        product = jnp.einsum('sbkvrn,cusbkn->sbkvcru', v_factors[sector], picked, precision=highest)
        real_part = product[:, :, :, 0, 0] - product[:, :, :, 1, 1]
        imag_part = product[:, :, :, 0, 1] + product[:, :, :, 1, 0]
        coeffs = jnp.stack([real_part, imag_part], 3)
        live_slot = (slot_ids[None, None, :] < block_count[sector][:, :, None]).astype(jnp.float32)
        return coeffs * live_slot[:, :, :, None, None, None]
    every_coeff = lax.map(sender, jnp.arange(N_AZIM, dtype=jnp.int32))

    def receiver(sector):
        arrived = jnp.transpose(jnp.take(every_coeff, sector, axis=2), (1, 0, 2, 3, 4, 5))
        product = jnp.einsum('sakqrn,sakcru->sakqcun', u_factors[sector], arrived, precision=highest)
        real_part = product[:, :, :, 0, 0] - product[:, :, :, 1, 1]
        imag_part = product[:, :, :, 0, 1] + product[:, :, :, 1, 0]
        pieces = jnp.stack([real_part, imag_part], 3)
        place_table = (row_cluster[sector][..., None] == jnp.arange(NSP, dtype=jnp.int32)).astype(jnp.float32)
        return jnp.einsum('sakw,sakcun->cuwn', place_table, pieces, precision=highest)
    sectors = lax.map(receiver, jnp.arange(N_AZIM, dtype=jnp.int32))
    return jnp.transpose(sectors, (1, 2, 3, 0, 4)).reshape(2, NRHS, NSP, NAZ)

def reference(field, positions, normals, areas, col_cluster, block_count, row_cluster, v_factors, u_factors):
    near_rows = near_field(field, positions, normals, areas)
    far_rows = far_field(field, col_cluster, block_count, row_cluster, v_factors, u_factors)
    return 0.5 * field + near_rows + far_rows
```

```python
import functools
import math

import jax
import jax.numpy as jnp
from jax import lax
from jax.experimental import pallas as pl
from jax.experimental.pallas import tpu as pltpu
from jax.sharding import PartitionSpec as P

wavenumber = 0.9
coupling = 1.1
f32 = jnp.float32
bf16 = jnp.bfloat16

SEG = 8
SIN_POLY = (4.44286798, -7.30744541, 3.59480208, -0.78440355)
COS_POLY = (1.41420408, -6.97764206, 5.71523842, -1.72834866)


def split_two(value):
    high = value.astype(bf16)
    return high, (value - high.astype(f32)).astype(bf16)


def dot_nt(left, right):
    return lax.dot_general(left, right, (((1,), (1,)), ((), ())), preferred_element_type=f32)


def segment_swap(value):
    rows = value.shape[1]
    row = lax.broadcasted_iota(jnp.int32, value.shape, 1)
    seg = lax.broadcasted_iota(jnp.int32, value.shape, 2) // SEG
    bit = 1
    while bit < rows:
        row_bit = (row // bit) % 2
        seg_bit = (seg // bit) % 2
        up = jnp.roll(jnp.roll(value, -bit, 1), SEG * bit, 2)
        down = jnp.roll(jnp.roll(value, bit, 1), -SEG * bit, 2)
        value = jnp.where(row_bit == seg_bit, value, jnp.where(row_bit == 0, up, down))
        bit *= 2
    return value


def pack_kernel(field_ref, pos_ref, nrm_ref, area_ref, out_ref, low_ref, high_ref):
    rhs = field_ref.shape[1]
    weight = area_ref[...] * (wavenumber / (2.0 * math.pi) / (4.0 * math.pi))
    parts = [field_ref[c, u] * weight for c in range(2) for u in range(rhs)]
    parts += [pos_ref[i] for i in range(3)] + [nrm_ref[i] for i in range(3)]
    packed = segment_swap(jnp.stack(parts, 0))
    blocks = out_ref.shape[0]
    for q in range(len(parts)):
        out_ref[:, q, :] = packed[q]
        low_ref[:, q, :] = packed[q, : low_ref.shape[0]]
        high_ref[:, q, :] = packed[q, blocks - high_ref.shape[0] :]


def send_kernel(chosen_ref, count_ref, field_ref, v_ref, out_ref, table_ref):
    step = pl.program_id(0)
    peers = out_ref.shape[0]
    rank = v_ref.shape[3]
    cap = v_ref.shape[1]
    width = field_ref.shape[3]

    @pl.when(step == 0)
    def _():
        for row in range(field_ref.shape[2]):
            pair = jnp.concatenate([field_ref[0, :, row, :], field_ref[1, :, row, :]], 1)
            high, low = split_two(pair)
            table_ref[row] = jnp.concatenate([high.astype(f32), low.astype(f32)], 0).astype(bf16)

    lane = lax.broadcasted_iota(jnp.int32, (8, 2 * rank * cap), 1)
    for i in range(peers):
        peer = step * peers + i
        wide = []
        for k in range(cap):
            re, im = v_ref[i, k, 0], v_ref[i, k, 1]
            wide += [jnp.concatenate([re, -im], 1), jnp.concatenate([im, re], 1)]
        high, low = split_two(jnp.concatenate(wide, 0))
        left = jnp.concatenate([table_ref[chosen_ref[peer * cap + k]] for k in range(cap)], 0)
        first = dot_nt(left, high)
        second = dot_nt(left, low)
        total = jnp.zeros((8, 2 * rank * cap), f32)
        for k in range(cap):
            part = first[16 * k : 16 * k + 8] + (first[16 * k + 8 : 16 * k + 16] + second[16 * k : 16 * k + 8])
            here = (lane // (2 * rank) == k) & (k < count_ref[peer])
            total = jnp.where(here, part, total)
        out_ref[i, :, : 2 * rank * cap] = total
        out_ref[i, :, 2 * rank * cap :] = jnp.zeros((8, width - 2 * rank * cap), f32)


def receive_kernel(target_ref, coef_ref, u_ref, out_ref):
    step = pl.program_id(0)
    peers = coef_ref.shape[0]
    cap, rank, width = u_ref.shape[1], u_ref.shape[3], u_ref.shape[4]
    used = 2 * rank * cap

    @pl.when(step == 0)
    def _():
        out_ref[...] = jnp.zeros_like(out_ref)

    coef = coef_ref[...].reshape(peers * 8, width)
    lane = lax.broadcasted_iota(jnp.int32, coef.shape, 1)
    is_im = (lane // rank) % 2 == 1
    real_row = jnp.where(is_im, -coef, coef)
    imag_row = jnp.where(is_im, jnp.roll(coef, rank, 1), jnp.roll(coef, -rank, 1))
    zero = jnp.zeros_like(coef)
    rows = []
    for k in range(cap):
        here = lane // (2 * rank) == k
        rows += [jnp.where(here, real_row, zero), jnp.where(here, imag_row, zero)]
    for i in range(peers):
        left = jnp.concatenate([r[8 * i : 8 * i + 8, :used] for r in rows], 0)
        left_high, left_low = split_two(left)
        high, low = split_two(u_ref[i].reshape(used, width))
        one = jnp.dot(jnp.concatenate([left_high, left_low], 0), high, preferred_element_type=f32)
        two = jnp.dot(left_high, low, preferred_element_type=f32)
        count = left.shape[0]
        total = one[:count] + (one[count:] + two)
        for k in range(cap):
            w = target_ref[(step * peers + i) * cap + k]
            out_ref[w] += total[16 * k : 16 * k + 16]


def near_kernel(left_ref, mid_ref, right_ref, field_ref, out_ref, pos_ref, wide_ref, kern_ref, acc_ref):
    blocks = mid_ref.shape[0]
    halo = left_ref.shape[0]
    window = 2 * halo + 1
    width = mid_ref.shape[2]
    turn = wavenumber / (2.0 * math.pi)

    def block_in(index):
        if index < halo:
            return left_ref.at[index]
        if index < halo + blocks:
            return mid_ref.at[index - halo]
        return right_ref.at[index - halo - blocks]

    origin = mid_ref[blocks // 2, 16:19, 0:1]
    for b in range(blocks + 2 * halo):
        ref = block_in(b)
        pos_ref[b, 0:3, :] = (ref[16:19, :] - origin) * turn
        pos_ref[b, 3:6, :] = ref[19:22, :]
        re, im = ref[0:8, :], ref[8:16, :]
        rows = jnp.concatenate(
            [jnp.concatenate([re, -im], 1), jnp.concatenate([im, re], 1)], 0
        )
        high, low = split_two(rows)
        wide_ref[:, 2 * width * b : 2 * width * (b + 1)] = jnp.concatenate([high, low], 0)

    chunk = 16
    sub = lax.broadcasted_iota(jnp.int32, (chunk, width), 0)
    lane = lax.broadcasted_iota(jnp.int32, (chunk, width), 1)

    def one_block(tb, carry):
        target = jnp.transpose(pos_ref[tb + halo])
        for ch in range(width // chunk):
            rows = slice(ch * chunk, (ch + 1) * chunk)
            tx, ty, tz = (
                jnp.broadcast_to(target[rows, i : i + 1], (chunk, width)) for i in range(3)
            )
            for d in range(window):
                src = pos_ref.at[tb + d]
                dx, dy, dz = tx - src[0:1, :], ty - src[1:2, :], tz - src[2:3, :]
                squared = dx * dx + dy * dy + dz * dz
                if d == halo:
                    self_pair = (sub + ch * chunk) == lane
                    squared = jnp.where(self_pair, 1.0, squared)
                inv = lax.rsqrt(squared)
                turns = squared * inv
                frac = turns - jnp.round(turns)
                z = frac * frac
                s = frac * (SIN_POLY[0] + z * (SIN_POLY[1] + z * (SIN_POLY[2] + z * SIN_POLY[3])))
                c = COS_POLY[0] + z * (COS_POLY[1] + z * (COS_POLY[2] + z * COS_POLY[3]))
                sine = s * c
                cosine = 1.0 - s * s
                if d == halo:
                    inv = jnp.where(self_pair, 0.0, inv)
                if d == 0:
                    inv = jnp.where(lane % SEG >= sub % SEG, inv, 0.0)
                if d == window - 1:
                    inv = jnp.where(lane % SEG <= sub % SEG, inv, 0.0)
                slant = (dx * src[3:4, :] + dy * src[4:5, :] + dz * src[5:6, :]) * inv
                first = (slant * turn) * inv
                second = wavenumber * slant + coupling
                pc, ps = inv * cosine, inv * sine
                k_re = first * pc + second * ps
                k_im = first * ps - second * pc
                for kern, at in ((k_re, 0), (k_im, width)):
                    high, low = split_two(kern)
                    cols = slice(2 * width * d + at, 2 * width * d + at + width)
                    kern_ref[ch * chunk : (ch + 1) * chunk, cols] = high
                    kern_ref[width + ch * chunk : width + (ch + 1) * chunk, cols] = low
        start = pl.multiple_of(tb * (2 * width), 2 * width)
        rhs = wide_ref[:, pl.ds(start, 2 * width * window)]
        prod = dot_nt(kern_ref[...], rhs)
        prod = prod[:width] + prod[width:]
        prod = jnp.transpose(prod)
        acc_ref[:, pl.ds(tb, 1), :] = (prod[:16] + prod[16:])[:, None, :]
        return carry

    lax.fori_loop(0, blocks, one_block, 0)
    swapped = segment_swap(acc_ref[...])
    rhs_count = field_ref.shape[1]
    for c in range(2):
        for u in range(rhs_count):
            out_ref[c, u] = swapped[c * rhs_count + u] + 0.5 * field_ref[c, u]


def whole(shape):
    return pl.BlockSpec(shape, lambda *_: (0,) * len(shape))


def run_pack(field, positions, normals, areas):
    rows, width = areas.shape
    blocks = width // SEG
    halo = blocks // 4
    shapes = [(blocks, 24, width), (halo, 24, width), (halo, 24, width)]
    return pl.pallas_call(
        pack_kernel,
        out_shape=[jax.ShapeDtypeStruct(s, f32) for s in shapes],
        name="pack",
    )(field, positions, normals, areas)


def run_send(chosen, counts, field, v):
    peers, cap, _, rank, width = v.shape
    step = 8
    grid_spec = pltpu.PrefetchScalarGridSpec(
        num_scalar_prefetch=2,
        grid=(peers // step,),
        in_specs=[
            pl.BlockSpec(field.shape, lambda i, *_: (0, 0, 0, 0)),
            pl.BlockSpec((step, cap, 2, rank, width), lambda i, *_: (i, 0, 0, 0, 0)),
        ],
        out_specs=pl.BlockSpec((step, 8, width), lambda i, *_: (i, 0, 0)),
        scratch_shapes=[pltpu.VMEM((field.shape[2], 16, 2 * width), bf16)],
    )
    return pl.pallas_call(
        send_kernel,
        grid_spec=grid_spec,
        out_shape=jax.ShapeDtypeStruct((peers, 8, width), f32),
        name="send",
    )(chosen, counts, field, v)


def run_receive(targets, coef, u, span_rows):
    peers, cap, _, rank, width = u.shape
    step = 8
    grid_spec = pltpu.PrefetchScalarGridSpec(
        num_scalar_prefetch=1,
        grid=(peers // step,),
        in_specs=[
            pl.BlockSpec((step, 8, width), lambda i, *_: (i, 0, 0)),
            pl.BlockSpec((step, cap, 2, rank, width), lambda i, *_: (i, 0, 0, 0, 0)),
        ],
        out_specs=pl.BlockSpec((span_rows, 16, width), lambda i, *_: (0, 0, 0)),
    )
    return pl.pallas_call(
        receive_kernel,
        grid_spec=grid_spec,
        out_shape=jax.ShapeDtypeStruct((span_rows, 16, width), f32),
        name="receive",
    )(targets, coef, u)


def run_near(left, mid, right, field):
    blocks, _, width = mid.shape
    halo = left.shape[0]
    count = blocks + 2 * halo
    return pl.pallas_call(
        near_kernel,
        out_shape=jax.ShapeDtypeStruct(field.shape, f32),
        scratch_shapes=[
            pltpu.VMEM((count, 8, width), f32),
            pltpu.VMEM((32, 2 * width * count), bf16),
            pltpu.VMEM((2 * width, 2 * width * (2 * halo + 1)), bf16),
            pltpu.VMEM((16, blocks, width), f32),
        ],
        compiler_params=pltpu.CompilerParams(vmem_limit_bytes=40 * 1024 * 1024),
        name="near",
    )(left, mid, right, field)


def shards(
    field, positions, normals, areas, col_cluster, block_count, row_cluster, v_factors, u_factors
):
    azim = lax.axis_size("azim")
    span = lax.axis_size("span")
    span_rows = field.shape[2]
    mid, low, high = run_pack(field, positions, normals, areas)
    forward = [(i, (i + 1) % azim) for i in range(azim)]
    backward = [(b, a) for a, b in forward]
    left = lax.ppermute(high, "azim", forward)
    right = lax.ppermute(low, "azim", backward)
    outgoing = run_send(
        col_cluster.reshape(-1), block_count.reshape(-1), field, v_factors.reshape(v_factors.shape[2:])
    )
    incoming = lax.all_to_all(outgoing, "azim", split_axis=0, concat_axis=0, tiled=True)
    near = run_near(left, mid, right, field)
    rows = run_receive(
        row_cluster.reshape(-1), incoming, u_factors.reshape(u_factors.shape[2:]), span * span_rows
    )
    me = lax.axis_index("span")
    total = lax.dynamic_slice_in_dim(rows, me * span_rows, span_rows, 0)
    for k in range(1, span):
        ring = [(i, (i + k) % span) for i in range(span)]
        other = ((me + k) % span) * span_rows
        piece = lax.dynamic_slice_in_dim(rows, other, span_rows, 0)
        total = total + lax.ppermute(piece, "span", ring)
    return near + total.transpose(1, 0, 2).reshape(near.shape)


def solution(mesh):
    placed = (
        P(None, None, "span", "azim"),
        P(None, "span", "azim"),
        P(None, "span", "azim"),
        P("span", "azim"),
        P("azim", "span", None, None),
        P("azim", "span", None),
        P("azim", "span", None, None),
        P("azim", "span", None, None, None, None, None),
        P("azim", "span", None, None, None, None, None),
    )
    return jax.shard_map(
        shards, mesh=mesh, in_specs=placed, out_specs=P(None, None, "span", "azim"), check_vma=False
    )
```

```python
import functools
import math

import jax
import jax.numpy as jnp
from jax import lax
from jax.experimental import pallas as pl
from jax.experimental.pallas import tpu as pltpu
from jax.sharding import PartitionSpec as P

wavenumber = 0.9
coupling = 1.1
f32 = jnp.float32
bf16 = jnp.bfloat16

SEG = 8
SIN_POLY = (4.44286798, -7.30744541, 3.59480208, -0.78440355)
COS_POLY = (1.41420408, -6.97764206, 5.71523842, -1.72834866)


def split_two(value):
    high = value.astype(bf16)
    return high, (value - high.astype(f32)).astype(bf16)


def dot_nt(left, right):
    return lax.dot_general(left, right, (((1,), (1,)), ((), ())), preferred_element_type=f32)


def segment_swap(value):
    rows = value.shape[1]
    row = lax.broadcasted_iota(jnp.int32, value.shape, 1)
    seg = lax.broadcasted_iota(jnp.int32, value.shape, 2) // SEG
    bit = 1
    while bit < rows:
        row_bit = (row // bit) % 2
        seg_bit = (seg // bit) % 2
        up = jnp.roll(jnp.roll(value, -bit, 1), SEG * bit, 2)
        down = jnp.roll(jnp.roll(value, bit, 1), -SEG * bit, 2)
        value = jnp.where(row_bit == seg_bit, value, jnp.where(row_bit == 0, up, down))
        bit *= 2
    return value


def pack_kernel(field_ref, pos_ref, nrm_ref, area_ref, out_ref, low_ref, high_ref):
    rhs = field_ref.shape[1]
    weight = area_ref[...] * (wavenumber / (2.0 * math.pi) / (4.0 * math.pi))
    parts = [field_ref[c, u] * weight for c in range(2) for u in range(rhs)]
    parts += [pos_ref[i] for i in range(3)] + [nrm_ref[i] for i in range(3)]
    packed = segment_swap(jnp.stack(parts, 0))
    blocks = out_ref.shape[0]
    for q in range(len(parts)):
        out_ref[:, q, :] = packed[q]
        low_ref[:, q, :] = packed[q, : low_ref.shape[0]]
        high_ref[:, q, :] = packed[q, blocks - high_ref.shape[0] :]


def send_kernel(chosen_ref, count_ref, field_ref, v_hbm, out_ref, v_ref, table_ref, sems):
    chunks = sems.shape[0]
    peers = out_ref.shape[0] // chunks
    rank = v_ref.shape[3]
    cap = v_ref.shape[1]
    width = out_ref.shape[2]
    span_rows = table_ref.shape[0]

    def fetch(index):
        rows = pl.ds(index * peers, peers)
        return pltpu.make_async_copy(v_hbm.at[rows], v_ref.at[rows], sems.at[index])

    for index in range(chunks):
        fetch(index).start()

    half = field_ref.shape[0] // 2
    for row in range(span_rows):
        pair = jnp.concatenate(
            [field_ref[pl.ds(c * half + row, 8, stride=span_rows), :] for c in range(2)], 1
        )
        high, low = split_two(pair)
        table_ref[row] = jnp.concatenate([high.astype(f32), low.astype(f32)], 0).astype(bf16)

    lane = lax.broadcasted_iota(jnp.int32, (8, 2 * rank * cap), 1)

    def one_chunk(index, carry):
        fetch(index).wait()
        for i in range(peers):
            peer = index * peers + i
            wide = []
            for k in range(cap):
                re, im = v_ref[peer, k, 0], v_ref[peer, k, 1]
                wide += [jnp.concatenate([re, -im], 1), jnp.concatenate([im, re], 1)]
            high, low = split_two(jnp.concatenate(wide, 0))
            left = jnp.concatenate([table_ref[chosen_ref[k, peer]] for k in range(cap)], 0)
            first = dot_nt(left, high)
            second = dot_nt(left, low)
            total = jnp.zeros((8, 2 * rank * cap), f32)
            for k in range(cap):
                at = 16 * k
                part = first[at : at + 8] + (first[at + 8 : at + 16] + second[at : at + 8])
                here = (lane // (2 * rank) == k) & (k < count_ref[0, peer])
                total = jnp.where(here, part, total)
            out_ref[peer, :, : 2 * rank * cap] = total
            out_ref[peer, :, 2 * rank * cap :] = jnp.zeros((8, width - 2 * rank * cap), f32)
        return carry

    lax.fori_loop(0, chunks, one_chunk, 0)


def receive_kernel(target_ref, me_ref, coef_ref, u_ref, *rest):
    outs, acc_ref = rest[:-1], rest[-1]
    span = len(outs)
    count, cap, rank, width = u_ref.shape[0], u_ref.shape[1], u_ref.shape[3], u_ref.shape[4]
    span_rows = outs[0].shape[1]
    used = 2 * rank * cap
    piece = acc_ref.shape[0] // span
    peers = 8
    acc_ref[...] = jnp.zeros_like(acc_ref)
    me = me_ref[0]
    lane = lax.broadcasted_iota(jnp.int32, (peers * 8, width), 1)

    def one_chunk(index, carry):
        coef = coef_ref[pl.ds(index * peers, peers)].reshape(peers * 8, width)
        is_im = (lane // rank) % 2 == 1
        real_row = jnp.where(is_im, -coef, coef)
        imag_row = jnp.where(is_im, jnp.roll(coef, rank, 1), jnp.roll(coef, -rank, 1))
        zero = jnp.zeros_like(coef)
        rows = []
        for k in range(cap):
            here = lane // (2 * rank) == k
            rows += [jnp.where(here, real_row, zero), jnp.where(here, imag_row, zero)]
        for i in range(peers):
            peer = index * peers + i
            left = jnp.concatenate([r[8 * i : 8 * i + 8, :used] for r in rows], 0)
            left_high, left_low = split_two(left)
            high, low = split_two(u_ref[peer].reshape(used, width))
            one = jnp.dot(
                jnp.concatenate([left_high, left_low], 0), high, preferred_element_type=f32
            )
            two = jnp.dot(left_high, low, preferred_element_type=f32)
            many = left.shape[0]
            total = one[:many] + (one[many:] + two)
            for k in range(cap):
                w = target_ref[k, peer]
                place = ((w // span_rows - me + span) % span) * piece + w % span_rows
                at = pl.ds(place, 16, stride=span_rows)
                acc_ref[at, :] += total[16 * k : 16 * k + 16]
        return carry

    lax.fori_loop(0, count // peers, one_chunk, 0)
    for k in range(span):
        outs[k][...] = acc_ref[k * piece : (k + 1) * piece, :].reshape(outs[k].shape)


def near_kernel(begin, count, skip, edge, *refs):
    if edge:
        left_ref, mid_ref, right_ref, done_ref, field_ref = refs[:5]
        out_ref, pos_ref, wide_ref, kern_ref, acc_ref = refs[5:]
    else:
        mid_ref, acc_ref, pos_ref, wide_ref, kern_ref = refs
    blocks = mid_ref.shape[0]
    halo = blocks // 4
    window = 2 * halo + 1
    width = mid_ref.shape[2]
    turn = wavenumber / (2.0 * math.pi)

    def block_in(index):
        if index < halo:
            return left_ref.at[index]
        if index < halo + blocks:
            return mid_ref.at[index - halo]
        return right_ref.at[index - halo - blocks]

    origin = mid_ref[blocks // 2, 16:19, 0:1]
    for b in range(0 if edge else halo, blocks + (2 if edge else 1) * halo):
        ref = block_in(b)
        pos_ref[b, 0:3, :] = (ref[16:19, :] - origin) * turn
        pos_ref[b, 3:6, :] = ref[19:22, :]
        re, im = ref[0:8, :], ref[8:16, :]
        rows = jnp.concatenate(
            [jnp.concatenate([re, -im], 1), jnp.concatenate([im, re], 1)], 0
        )
        high, low = split_two(rows)
        wide_ref[:, 2 * width * b : 2 * width * (b + 1)] = jnp.concatenate([high, low], 0)

    chunk = 16
    sub = lax.broadcasted_iota(jnp.int32, (chunk, width), 0)
    lane = lax.broadcasted_iota(jnp.int32, (chunk, width), 1)

    def one_block(step, carry):
        tb = jnp.where(step < count, step, step + skip) + begin
        target = jnp.transpose(pos_ref[tb + halo])
        for ch in range(width // chunk):
            rows = slice(ch * chunk, (ch + 1) * chunk)
            tx, ty, tz = (
                jnp.broadcast_to(target[rows, i : i + 1], (chunk, width)) for i in range(3)
            )
            for d in range(window):
                src = pos_ref.at[tb + d]
                dx, dy, dz = tx - src[0:1, :], ty - src[1:2, :], tz - src[2:3, :]
                squared = dx * dx + dy * dy + dz * dz
                if d == halo:
                    self_pair = (sub + ch * chunk) == lane
                    squared = jnp.where(self_pair, 1.0, squared)
                inv = lax.rsqrt(squared)
                turns = squared * inv
                frac = turns - jnp.round(turns)
                z = frac * frac
                s = frac * (SIN_POLY[0] + z * (SIN_POLY[1] + z * (SIN_POLY[2] + z * SIN_POLY[3])))
                c = COS_POLY[0] + z * (COS_POLY[1] + z * (COS_POLY[2] + z * COS_POLY[3]))
                sine = s * c
                cosine = 1.0 - s * s
                if d == halo:
                    inv = jnp.where(self_pair, 0.0, inv)
                if d == 0:
                    inv = jnp.where(lane % SEG >= sub % SEG, inv, 0.0)
                if d == window - 1:
                    inv = jnp.where(lane % SEG <= sub % SEG, inv, 0.0)
                slant = (dx * src[3:4, :] + dy * src[4:5, :] + dz * src[5:6, :]) * inv
                first = (slant * turn) * inv
                second = wavenumber * slant + coupling
                pc, ps = inv * cosine, inv * sine
                k_re = first * pc + second * ps
                k_im = first * ps - second * pc
                for kern, at in ((k_re, 0), (k_im, width)):
                    high, low = split_two(kern)
                    cols = slice(2 * width * d + at, 2 * width * d + at + width)
                    kern_ref[ch * chunk : (ch + 1) * chunk, cols] = high
                    kern_ref[width + ch * chunk : width + (ch + 1) * chunk, cols] = low
        start = pl.multiple_of(tb * (2 * width), 2 * width)
        rhs = wide_ref[:, pl.ds(start, 2 * width * window)]
        prod = dot_nt(kern_ref[...], rhs)
        prod = prod[:width] + prod[width:]
        prod = jnp.transpose(prod)
        at = tb if edge else step
        acc_ref[:, pl.ds(at, 1), :] = (prod[:16] + prod[16:])[:, None, :]
        return carry

    lax.fori_loop(0, 2 * count if edge else count, one_block, 0)
    if edge:
        acc_ref[:, count : count + skip, :] = done_ref[...]
        swapped = segment_swap(acc_ref[...])
        rhs_count = field_ref.shape[1]
        for c in range(2):
            for u in range(rhs_count):
                out_ref[c, u] = swapped[c * rhs_count + u] + 0.5 * field_ref[c, u]


def run_pack(field, positions, normals, areas):
    rows, width = areas.shape
    blocks = width // SEG
    halo = blocks // 4
    shapes = [(blocks, 24, width), (halo, 24, width), (halo, 24, width)]
    return pl.pallas_call(
        pack_kernel,
        out_shape=[jax.ShapeDtypeStruct(s, f32) for s in shapes],
        cost_estimate=cost(10**8, 10**6),
        name="pack",
    )(field, positions, normals, areas)


def vmem(count=1):
    return [pl.BlockSpec(memory_space=pltpu.VMEM)] * count


def smem(count=1):
    return [pl.BlockSpec(memory_space=pltpu.SMEM)] * count


def cost(flops, size):
    return pl.CostEstimate(flops=flops, bytes_accessed=size, transcendentals=0)


def run_send(chosen, counts, field, v):
    peers, cap, _, rank, width = v.shape
    rhs, span_rows = field.shape[1:3]
    chunks = 8
    return pl.pallas_call(
        send_kernel,
        in_specs=smem(2) + vmem(1) + [pl.BlockSpec(memory_space=pl.ANY)],
        out_specs=vmem()[0],
        out_shape=jax.ShapeDtypeStruct((peers, 8, width), f32),
        scratch_shapes=[
            pltpu.VMEM(v.shape, f32),
            pltpu.VMEM((span_rows, 16, 2 * width), bf16),
            pltpu.SemaphoreType.DMA((chunks,)),
        ],
        cost_estimate=cost(3 * 10**9, 4 * v.size),
        name="send",
    )(chosen, counts, field.reshape(2 * rhs * span_rows, width), v)


def run_receive(targets, me, coef, u, span, span_rows):
    width = u.shape[4]
    shape = (16, span_rows, width)
    return pl.pallas_call(
        receive_kernel,
        in_specs=smem(2) + vmem(2),
        out_specs=vmem(span),
        out_shape=[jax.ShapeDtypeStruct(shape, f32)] * span,
        scratch_shapes=[pltpu.VMEM((span * 16 * span_rows, width), f32)],
        cost_estimate=cost(3 * 10**9, 4 * u.size),
        name="receive",
    )(targets, me, coef, u)


def near_scratch(blocks, width):
    halo = blocks // 4
    count = blocks + 2 * halo
    return [
        pltpu.VMEM((count, 8, width), f32),
        pltpu.VMEM((32, 2 * width * count), bf16),
        pltpu.VMEM((2 * width, 2 * width * (2 * halo + 1)), bf16),
    ]


def run_near_inner(mid):
    blocks, _, width = mid.shape
    halo = blocks // 4
    count = blocks - 2 * halo
    return pl.pallas_call(
        functools.partial(near_kernel, halo, count, 0, False),
        in_specs=vmem(1),
        out_specs=vmem()[0],
        out_shape=jax.ShapeDtypeStruct((16, count, width), f32),
        scratch_shapes=near_scratch(blocks, width),
        cost_estimate=cost(10**10, 10**6),
        name="near_inner",
    )(mid)


def run_near_edge(left, mid, right, done, field):
    blocks, _, width = mid.shape
    halo = left.shape[0]
    return pl.pallas_call(
        functools.partial(near_kernel, 0, halo, blocks - 2 * halo, True),
        in_specs=vmem(5),
        out_specs=vmem()[0],
        out_shape=jax.ShapeDtypeStruct(field.shape, f32),
        scratch_shapes=near_scratch(blocks, width) + [pltpu.VMEM((16, blocks, width), f32)],
        cost_estimate=cost(10**10, 10**6),
        name="near_edge",
    )(left, mid, right, done, field)


def shards(
    field, positions, normals, areas, col_cluster, block_count, row_cluster, v_factors, u_factors
):
    azim = lax.axis_size("azim")
    span = lax.axis_size("span")
    span_rows = field.shape[2]
    hold = lax.optimization_barrier
    outgoing = run_send(
        col_cluster[0, 0].T, block_count[0], field, v_factors.reshape(v_factors.shape[2:])
    )
    outgoing, positions = hold((outgoing, positions))
    incoming = lax.all_to_all(outgoing, "azim", split_axis=0, concat_axis=0, tiled=True)
    mid, low, high = run_pack(field, positions, normals, areas)
    forward = [(i, (i + 1) % azim) for i in range(azim)]
    backward = [(b, a) for a, b in forward]
    left = lax.ppermute(high, "azim", forward)
    right = lax.ppermute(low, "azim", backward)
    inner = run_near_inner(mid)
    incoming, inner, left, right = hold((incoming, inner, left, right))
    me = lax.axis_index("span").astype(jnp.int32).reshape(1)
    pieces = run_receive(
        row_cluster[0, 0].T, me, incoming, u_factors.reshape(u_factors.shape[2:]), span, span_rows
    )
    mid, *pieces = hold((mid, *pieces))
    total = pieces[0]
    others = []
    for k in range(1, span):
        ring = [(i, (i + k) % span) for i in range(span)]
        others.append(lax.ppermute(pieces[k], "span", ring))
    near = run_near_edge(left, mid, right, inner, field)
    for other in others:
        total = total + other
    return near + total.reshape(near.shape)


def solution(mesh):
    placed = (
        P(None, None, "span", "azim"),
        P(None, "span", "azim"),
        P(None, "span", "azim"),
        P("span", "azim"),
        P("azim", "span", None, None),
        P("azim", "span", None),
        P("azim", "span", None, None),
        P("azim", "span", None, None, None, None, None),
        P("azim", "span", None, None, None, None, None),
    )
    return jax.shard_map(
        shards, mesh=mesh, in_specs=placed, out_specs=P(None, None, "span", "azim"), check_vma=False
    )
```

```python
import functools
import math

import jax
import jax.numpy as jnp
from jax import lax
from jax.experimental import pallas as pl
from jax.experimental.pallas import tpu as pltpu
from jax.sharding import PartitionSpec as P

wavenumber = 0.9
coupling = 1.1
f32 = jnp.float32
bf16 = jnp.bfloat16

SEG = 8
SIN_POLY = (2.2214303951, -0.9131751650, 0.1098397679)


def split_two(value):
    high = value.astype(bf16)
    return high, (value - high.astype(f32)).astype(bf16)


def split_three(value):
    high = value.astype(bf16).astype(f32)
    rest = value - high
    middle = rest.astype(bf16).astype(f32)
    return high, middle, rest - middle


def dot_nt(left, right):
    return lax.dot_general(left, right, (((1,), (1,)), ((), ())), preferred_element_type=f32)


def segment_swap(value):
    rows = value.shape[1]
    row = lax.broadcasted_iota(jnp.int32, value.shape, 1)
    seg = lax.broadcasted_iota(jnp.int32, value.shape, 2) // SEG
    bit = 1
    while bit < rows:
        row_bit = (row // bit) % 2
        seg_bit = (seg // bit) % 2
        up = jnp.roll(jnp.roll(value, -bit, 1), SEG * bit, 2)
        down = jnp.roll(jnp.roll(value, bit, 1), -SEG * bit, 2)
        value = jnp.where(row_bit == seg_bit, value, jnp.where(row_bit == 0, up, down))
        bit *= 2
    return value


def pack(field_ref, pos_ref, nrm_ref, area_ref, out_ref, low_ref, high_ref):
    span_rows, width = area_ref.shape
    weight = area_ref[...] * (wavenumber / (2.0 * math.pi) / (4.0 * math.pi))
    field = field_ref[...].reshape(field_ref.shape[0] // span_rows, span_rows, width)
    parts = [field[q] * weight for q in range(field.shape[0])]
    parts += [pos_ref[i] for i in range(3)] + [nrm_ref[i] for i in range(3)]
    packed = segment_swap(jnp.stack(parts, 0))
    blocks = out_ref.shape[0]
    for q in range(len(parts)):
        out_ref[:, q, :] = packed[q]
        low_ref[:, q, :] = packed[q, : low_ref.shape[0]]
        high_ref[:, q, :] = packed[q, blocks - high_ref.shape[0] :]


def send_kernel(chosen_ref, count_ref, field_ref, pos_ref, nrm_ref, area_ref, v_hbm, *rest):
    out_ref, mid_ref, low_ref, high_ref, v_ref, table_ref, sems = rest
    chunks = sems.shape[0]
    peers = out_ref.shape[0] // chunks
    rank = v_ref.shape[3]
    cap = v_ref.shape[1]
    width = out_ref.shape[2]
    span_rows = table_ref.shape[0]

    def fetch(index):
        rows = pl.ds(index * peers, peers)
        return pltpu.make_async_copy(v_hbm.at[rows], v_ref.at[rows], sems.at[index])

    for index in range(chunks):
        fetch(index).start()
    pack(field_ref, pos_ref, nrm_ref, area_ref, mid_ref, low_ref, high_ref)

    half = field_ref.shape[0] // 2
    for row in range(span_rows):
        pair = jnp.concatenate(
            [field_ref[pl.ds(c * half + row, 8, stride=span_rows), :] for c in range(2)], 1
        )
        high, low = split_two(pair)
        table_ref[row] = jnp.concatenate([high.astype(f32), low.astype(f32)], 0).astype(bf16)

    lane = lax.broadcasted_iota(jnp.int32, (8, 2 * rank * cap), 1)

    def one_chunk(index, carry):
        fetch(index).wait()
        for i in range(peers):
            peer = index * peers + i
            wide = []
            for k in range(cap):
                re, im = v_ref[peer, k, 0], v_ref[peer, k, 1]
                wide += [jnp.concatenate([re, -im], 1), jnp.concatenate([im, re], 1)]
            high, low = split_two(jnp.concatenate(wide, 0))
            left = jnp.concatenate([table_ref[chosen_ref[k, peer]] for k in range(cap)], 0)
            first = dot_nt(left, high)
            second = dot_nt(left, low)
            total = jnp.zeros((8, 2 * rank * cap), f32)
            for k in range(cap):
                at = 16 * k
                part = first[at : at + 8] + (first[at + 8 : at + 16] + second[at : at + 8])
                here = (lane // (2 * rank) == k) & (k < count_ref[0, peer])
                total = jnp.where(here, part, total)
            out_ref[peer, :, : 2 * rank * cap] = total
            out_ref[peer, :, 2 * rank * cap :] = jnp.zeros((8, width - 2 * rank * cap), f32)
        return carry

    lax.fori_loop(0, chunks, one_chunk, 0)


def receive_kernel(target_ref, me_ref, coef_ref, u_ref, *rest):
    outs, accs = rest[:-4], rest[-4:]
    span = len(outs)
    count, cap, rank, width = u_ref.shape[0], u_ref.shape[1], u_ref.shape[3], u_ref.shape[4]
    span_rows = outs[0].shape[1]
    used = 2 * rank * cap
    piece = accs[0].shape[0] // span
    peers = 8
    for acc_ref in accs:
        acc_ref[...] = jnp.zeros_like(acc_ref)
    me = me_ref[0]
    lane = lax.broadcasted_iota(jnp.int32, (peers * 8, width), 1)

    def one_chunk(index, carry):
        coef = coef_ref[pl.ds(index * peers, peers)].reshape(peers * 8, width)
        is_im = (lane // rank) % 2 == 1
        real_row = jnp.where(is_im, -coef, coef)
        imag_row = jnp.where(is_im, jnp.roll(coef, rank, 1), jnp.roll(coef, -rank, 1))
        zero = jnp.zeros_like(coef)
        rows = []
        for k in range(cap):
            here = lane // (2 * rank) == k
            rows += [jnp.where(here, real_row, zero), jnp.where(here, imag_row, zero)]
        for i in range(peers):
            peer = index * peers + i
            left = jnp.concatenate([r[8 * i : 8 * i + 8, :used] for r in rows], 0)
            left_high, left_low = split_two(left)
            high, low = split_two(u_ref[peer].reshape(used, width))
            one = jnp.dot(
                jnp.concatenate([left_high, left_low], 0), high, preferred_element_type=f32
            )
            two = jnp.dot(left_high, low, preferred_element_type=f32)
            many = left.shape[0]
            total = one[:many] + (one[many:] + two)
            for k in range(cap):
                w = target_ref[k, peer]
                place = ((w // span_rows - me + span) % span) * piece + w % span_rows
                at = pl.ds(place, 16, stride=span_rows)
                acc_ref = accs[(2 * i + k) % 4]
                acc_ref[at, :] += total[16 * k : 16 * k + 16]
        return carry

    lax.fori_loop(0, count // peers, one_chunk, 0)
    for k in range(span):
        at = slice(k * piece, (k + 1) * piece)
        total = (accs[0][at, :] + accs[1][at, :]) + (accs[2][at, :] + accs[3][at, :])
        outs[k][...] = total.reshape(outs[k].shape)


def near_kernel(begin, count, skip, edge, *refs):
    scratch = refs[-7:]
    pos_ref, wide_ref, kern_even, kern_odd, target_ref, source_ref, acc_ref = scratch
    if edge:
        left_ref, mid_ref, right_ref, done_ref, field_ref, out_ref = refs[:-7]
    else:
        mid_ref, out_ref = refs[:-7]
    blocks = mid_ref.shape[0]
    halo = blocks // 4
    window = 2 * halo + 1
    width = mid_ref.shape[2]
    turn = wavenumber / (2.0 * math.pi)

    def block_in(index):
        if index < halo:
            return left_ref.at[index]
        if index < halo + blocks:
            return mid_ref.at[index - halo]
        return right_ref.at[index - halo - blocks]

    origin = mid_ref[blocks // 2, 16:19, 0:1]
    row = lax.broadcasted_iota(jnp.int32, (8, width), 0)
    for b in range(0 if edge else halo, blocks + (2 if edge else 1) * halo):
        ref = block_in(b)
        pad = jnp.zeros((5, width), f32)
        pos_ref[b, 0:8, :] = jnp.concatenate([(ref[16:19, :] - origin) * turn, pad], 0)
        pos_ref[b, 8:16, :] = jnp.concatenate([ref[19:22, :] * wavenumber, pad], 0)
        re, im = ref[0:8, :], ref[8:16, :]
        rows = jnp.concatenate(
            [jnp.concatenate([re, -im], 1), jnp.concatenate([im, re], 1)], 0
        )
        high, low = split_two(rows)
        wide_ref[:, 2 * width * b : 2 * width * (b + 1)] = jnp.concatenate([high, low], 0)
    sources = window + 1
    zeros = jnp.zeros((width, 2 * width), bf16)
    for kern_ref in (kern_even, kern_odd):
        for part in (0, 2):
            kern_ref[(part + 1) * width : (part + 2) * width, : 2 * width] = zeros
            kern_ref[part * width : (part + 1) * width, 2 * width * (sources - 1) :] = zeros

    chunk = 16
    sub = lax.broadcasted_iota(jnp.int32, (chunk, width), 0)
    lane = lax.broadcasted_iota(jnp.int32, (chunk, width), 1)

    def evaluate(squared, num, at, offset):
        if offset == 0:
            self_pair = (sub + at) == lane
            squared = jnp.where(self_pair, 1.0, squared)
        inv = lax.rsqrt(squared)
        turns = squared * inv
        frac = turns - jnp.round(turns)
        z = frac * frac
        s1 = frac * (SIN_POLY[0] + z * (SIN_POLY[1] + z * SIN_POLY[2]))
        s1_sq = s1 * s1
        c1_sq = 2.0 - s1_sq
        s2 = s1 * (c1_sq * lax.rsqrt(c1_sq))
        c2 = c1_sq - s1_sq
        sine = s2 * c2
        cosine = 1.0 - s2 * (s2 + s2)
        if offset == 0:
            inv = jnp.where(self_pair, 0.0, inv)
        if offset == -halo:
            inv = jnp.where(lane % SEG >= sub % SEG, inv, 0.0)
        if offset == halo:
            inv = jnp.where(lane % SEG <= sub % SEG, inv, 0.0)
        slant = num * inv
        first = (slant * (turn / wavenumber)) * inv
        second = slant + coupling
        pc, ps = inv * cosine, inv * sine
        return first * pc + second * ps, first * ps - second * pc

    def pair_of(step):
        return jnp.where(step < count, step, step + skip) + begin

    def prepare(step, carry):
        tp = pair_of(step)
        center = pos_ref[2 * tp + halo, 0:8, 8 * SEG - 1 : 8 * SEG]

        def local_of(index):
            place = pos_ref[2 * tp + index, 0:8, :] - center
            return place, jnp.sum(place * place, axis=0, keepdims=True)

        for t in range(2):
            place, norm = local_of(halo + t)
            high, mid, low = split_three(
                jnp.where(row < 3, place, jnp.where(row == 3, 1.0, jnp.where(row == 4, norm, 0.0)))
            )
            rows = jnp.transpose(jnp.concatenate([high, high, mid, high, mid, low], 0))
            target_ref[step, t * width : (t + 1) * width, :] = rows.astype(bf16)
        for sb in range(sources):
            place, norm = local_of(sb)
            normal = pos_ref[2 * tp + sb, 8:16, :]
            along = jnp.sum(normal * place, axis=0, keepdims=True)
            wide = []
            for rows in (
                jnp.where(
                    row < 3, -2.0 * place, jnp.where(row == 3, norm, jnp.where(row == 4, 1.0, 0.0))
                ),
                jnp.where(row < 3, normal, jnp.where(row == 3, -along, 0.0)),
            ):
                high, mid, low = split_three(rows)
                wide.append(jnp.concatenate([high, mid, high, low, mid, high], 0))
            cols = slice(2 * width * sb, 2 * width * (sb + 1))
            source_ref[step, :, cols] = jnp.concatenate(wide, 1).astype(bf16)
        return carry

    def pair_kernels(step, kern_ref):
        for sb in range(sources):
            start = width if sb == sources - 1 else 0
            stop = width if sb == 0 else 2 * width
            gram = jnp.dot(
                target_ref[step, start:stop, :],
                source_ref[step, :, 2 * width * sb : 2 * width * (sb + 1)],
                preferred_element_type=f32,
            )
            for at in range(start, stop, chunk):
                t = at // width
                part = gram[at - start : at - start + chunk]
                kern = evaluate(part[:, :width], part[:, width:], at % width, sb - halo - t)
                for value, shift in zip(kern, (0, width)):
                    high, low = split_two(value)
                    cols = slice(2 * width * sb + shift, 2 * width * sb + shift + width)
                    kern_ref[at : at + chunk, cols] = high
                    kern_ref[2 * width + at : 2 * width + at + chunk, cols] = low

    def pair_sums(step, slot, kern_ref):
        start = pl.multiple_of(pair_of(step) * (4 * width), 4 * width)
        rhs = wide_ref[:, pl.ds(start, 2 * width * sources)]
        prod = dot_nt(kern_ref[...], rhs)
        prod = prod[: 2 * width] + prod[2 * width :]
        for t in range(2):
            half = jnp.transpose(prod[t * width : (t + 1) * width])
            acc_ref[:, pl.ds(2 * slot + t, 1), :] = (half[:16] + half[16:])[:, None, :]

    pairs = 2 * count if edge else count
    spare = acc_ref.shape[1] // 2 - 1

    def slot_of(step):
        return pair_of(step) if edge else step

    def two_pairs(index, carry):
        last = jnp.maximum(2 * index - 1, 0)
        pair_sums(last, jnp.where(index == 0, spare, slot_of(last)), kern_odd)
        pair_kernels(2 * index, kern_even)
        pair_sums(2 * index, slot_of(2 * index), kern_even)
        pair_kernels(2 * index + 1, kern_odd)
        return carry

    kern_odd[...] = jnp.zeros_like(kern_odd)
    lax.fori_loop(0, pairs, prepare, 0)
    lax.fori_loop(0, pairs // 2, two_pairs, 0)
    pair_sums(pairs - 1, slot_of(pairs - 1), kern_odd)
    if edge:
        acc_ref[:, 2 * count : 2 * (count + skip), :] = done_ref[...]
        swapped = segment_swap(acc_ref[:, :blocks, :])
        rhs_count = field_ref.shape[1]
        for c in range(2):
            for u in range(rhs_count):
                out_ref[c, u] = swapped[c * rhs_count + u] + 0.5 * field_ref[c, u]
    else:
        out_ref[...] = acc_ref[:, : 2 * pairs, :]


def vmem(count=1):
    return [pl.BlockSpec(memory_space=pltpu.VMEM)] * count


def smem(count=1):
    return [pl.BlockSpec(memory_space=pltpu.SMEM)] * count


def cost(flops, size):
    return pl.CostEstimate(flops=flops, bytes_accessed=size, transcendentals=0)


def params(megabytes):
    return pltpu.CompilerParams(vmem_limit_bytes=megabytes * 1024 * 1024)


def run_send(chosen, counts, field, positions, normals, areas, v):
    peers, cap, _, rank, width = v.shape
    rhs, span_rows = field.shape[1:3]
    chunks = 8
    blocks = width // SEG
    halo = blocks // 4
    shapes = [(peers, 8, width), (blocks, 24, width), (halo, 24, width), (halo, 24, width)]
    return pl.pallas_call(
        send_kernel,
        in_specs=smem(2) + vmem(4) + [pl.BlockSpec(memory_space=pl.ANY)],
        out_specs=vmem(4),
        out_shape=[jax.ShapeDtypeStruct(s, f32) for s in shapes],
        scratch_shapes=[
            pltpu.VMEM(v.shape, f32),
            pltpu.VMEM((span_rows, 16, 2 * width), bf16),
            pltpu.SemaphoreType.DMA((chunks,)),
        ],
        cost_estimate=cost(3 * 10**9, 4 * v.size),
        compiler_params=params(56),
        name="send",
    )(chosen, counts, field.reshape(2 * rhs * span_rows, width), positions, normals, areas, v)


def run_receive(targets, me, coef, u, span, span_rows):
    width = u.shape[4]
    shape = (16, span_rows, width)
    return pl.pallas_call(
        receive_kernel,
        in_specs=smem(2) + vmem(2),
        out_specs=vmem(span),
        out_shape=[jax.ShapeDtypeStruct(shape, f32)] * span,
        scratch_shapes=[pltpu.VMEM((span * 16 * span_rows, width), f32)] * 4,
        cost_estimate=cost(3 * 10**9, 4 * u.size),
        compiler_params=params(12),
        name="receive",
    )(targets, me, coef, u)


def near_scratch(blocks, width, pairs, slots):
    halo = blocks // 4
    count = blocks + 2 * halo
    span = 2 * width * (2 * halo + 2)
    return [
        pltpu.VMEM((count, 16, width), f32),
        pltpu.VMEM((32, 2 * width * count), bf16),
        pltpu.VMEM((4 * width, span), bf16),
        pltpu.VMEM((4 * width, span), bf16),
        pltpu.VMEM((pairs, 2 * width, 48), bf16),
        pltpu.VMEM((pairs, 48, span), bf16),
        pltpu.VMEM((16, 2 * slots + 2, width), f32),
    ]


def run_near_inner(mid):
    blocks, _, width = mid.shape
    halo = blocks // 4
    count = blocks - 2 * halo
    return pl.pallas_call(
        functools.partial(near_kernel, halo // 2, count // 2, 0, False),
        in_specs=vmem(1),
        out_specs=vmem()[0],
        out_shape=jax.ShapeDtypeStruct((16, count, width), f32),
        scratch_shapes=near_scratch(blocks, width, count // 2, count // 2),
        compiler_params=params(20),
        cost_estimate=cost(10**10, 10**6),
        name="near_inner",
    )(mid)


def run_near_edge(left, mid, right, done, field):
    blocks, _, width = mid.shape
    halo = left.shape[0]
    return pl.pallas_call(
        functools.partial(near_kernel, 0, halo // 2, blocks // 2 - halo, True),
        in_specs=vmem(5),
        out_specs=vmem()[0],
        out_shape=jax.ShapeDtypeStruct(field.shape, f32),
        scratch_shapes=near_scratch(blocks, width, halo, blocks // 2),
        compiler_params=params(20),
        cost_estimate=cost(10**10, 10**6),
        name="near_edge",
    )(left, mid, right, done, field)


def shards(
    field, positions, normals, areas, col_cluster, block_count, row_cluster, v_factors, u_factors
):
    azim = lax.axis_size("azim")
    span = lax.axis_size("span")
    span_rows = field.shape[2]
    hold = lax.optimization_barrier
    outgoing, mid, low, high = run_send(
        col_cluster[0, 0].T,
        block_count[0],
        field,
        positions,
        normals,
        areas,
        v_factors.reshape(v_factors.shape[2:]),
    )
    incoming = lax.all_to_all(outgoing, "azim", split_axis=0, concat_axis=0, tiled=True)
    forward = [(i, (i + 1) % azim) for i in range(azim)]
    backward = [(b, a) for a, b in forward]
    left = lax.ppermute(high, "azim", forward)
    right = lax.ppermute(low, "azim", backward)
    inner = run_near_inner(mid)
    incoming, inner, left, right = hold((incoming, inner, left, right))
    me = lax.axis_index("span").astype(jnp.int32).reshape(1)
    pieces = run_receive(
        row_cluster[0, 0].T, me, incoming, u_factors.reshape(u_factors.shape[2:]), span, span_rows
    )
    mid, *pieces = hold((mid, *pieces))
    total = pieces[0]
    others = []
    for k in range(1, span):
        ring = [(i, (i + k) % span) for i in range(span)]
        others.append(lax.ppermute(pieces[k], "span", ring))
    near = run_near_edge(left, mid, right, inner, field)
    for other in others:
        total = total + other
    return near + total.reshape(near.shape)


def solution(mesh):
    placed = (
        P(None, None, "span", "azim"),
        P(None, "span", "azim"),
        P(None, "span", "azim"),
        P("span", "azim"),
        P("azim", "span", None, None),
        P("azim", "span", None),
        P("azim", "span", None, None),
        P("azim", "span", None, None, None, None, None),
        P("azim", "span", None, None, None, None, None),
    )
    return jax.shard_map(
        shards, mesh=mesh, in_specs=placed, out_specs=P(None, None, "span", "azim"), check_vma=False
    )
```

```python
import functools
import math

import jax
import jax.numpy as jnp
from jax import lax
from jax.experimental import pallas as pl
from jax.experimental.pallas import tpu as pltpu
from jax.sharding import PartitionSpec as P

wavenumber = 0.9
coupling = 1.1
f32 = jnp.float32
bf16 = jnp.bfloat16

SEG = 8
SIN_POLY = (2.2214303951, -0.9131751650, 0.1098397679)


def split_two(value):
    high = value.astype(bf16)
    return high, (value - high.astype(f32)).astype(bf16)


def split_three(value):
    high = value.astype(bf16).astype(f32)
    rest = value - high
    middle = rest.astype(bf16).astype(f32)
    return high, middle, rest - middle


def dot_nt(left, right):
    return lax.dot_general(left, right, (((1,), (1,)), ((), ())), preferred_element_type=f32)


def segment_swap(value):
    rows = value.shape[1]
    row = lax.broadcasted_iota(jnp.int32, value.shape, 1)
    seg = lax.broadcasted_iota(jnp.int32, value.shape, 2) // SEG
    bit = 1
    while bit < rows:
        row_bit = (row // bit) % 2
        seg_bit = (seg // bit) % 2
        up = jnp.roll(jnp.roll(value, -bit, 1), SEG * bit, 2)
        down = jnp.roll(jnp.roll(value, bit, 1), -SEG * bit, 2)
        value = jnp.where(row_bit == seg_bit, value, jnp.where(row_bit == 0, up, down))
        bit *= 2
    return value


def pack(field_ref, pos_ref, nrm_ref, area_ref, out_ref, low_ref, high_ref):
    span_rows, width = area_ref.shape
    weight = area_ref[...] * (wavenumber / (2.0 * math.pi) / (4.0 * math.pi))
    field = field_ref[...].reshape(field_ref.shape[0] // span_rows, span_rows, width)
    parts = [field[q] * weight for q in range(field.shape[0])]
    parts += [pos_ref[i] for i in range(3)] + [nrm_ref[i] for i in range(3)]
    packed = segment_swap(jnp.stack(parts, 0))
    blocks = out_ref.shape[0]
    for q in range(len(parts)):
        out_ref[:, q, :] = packed[q]
        low_ref[:, q, :] = packed[q, : low_ref.shape[0]]
        high_ref[:, q, :] = packed[q, blocks - high_ref.shape[0] :]


def send_kernel(chosen_ref, count_ref, field_ref, pos_ref, nrm_ref, area_ref, v_hbm, *rest):
    out_ref, mid_ref, low_ref, high_ref, v_ref, table_ref, sems = rest
    chunks = sems.shape[0]
    peers = out_ref.shape[0] // chunks
    rank = v_ref.shape[3]
    cap = v_ref.shape[1]
    width = out_ref.shape[2]
    span_rows = table_ref.shape[0]

    def fetch(index):
        rows = pl.ds(index * peers, peers)
        return pltpu.make_async_copy(v_hbm.at[rows], v_ref.at[rows], sems.at[index])

    for index in range(chunks):
        fetch(index).start()
    pack(field_ref, pos_ref, nrm_ref, area_ref, mid_ref, low_ref, high_ref)

    half = field_ref.shape[0] // 2
    for row in range(span_rows):
        pair = jnp.concatenate(
            [field_ref[pl.ds(c * half + row, 8, stride=span_rows), :] for c in range(2)], 1
        )
        high, low = split_two(pair)
        table_ref[row] = jnp.concatenate([high.astype(f32), low.astype(f32)], 0).astype(bf16)

    lane = lax.broadcasted_iota(jnp.int32, (8, 2 * rank * cap), 1)

    def one_chunk(index, carry):
        fetch(index).wait()
        for i in range(peers):
            peer = index * peers + i
            wide = []
            for k in range(cap):
                re, im = v_ref[peer, k, 0], v_ref[peer, k, 1]
                wide += [jnp.concatenate([re, -im], 1), jnp.concatenate([im, re], 1)]
            high, low = split_two(jnp.concatenate(wide, 0))
            left = jnp.concatenate([table_ref[chosen_ref[k, peer]] for k in range(cap)], 0)
            first = dot_nt(left, high)
            second = dot_nt(left, low)
            total = jnp.zeros((8, 2 * rank * cap), f32)
            for k in range(cap):
                at = 16 * k
                part = first[at : at + 8] + (first[at + 8 : at + 16] + second[at : at + 8])
                here = (lane // (2 * rank) == k) & (k < count_ref[0, peer])
                total = jnp.where(here, part, total)
            out_ref[peer, :, : 2 * rank * cap] = total
            out_ref[peer, :, 2 * rank * cap :] = jnp.zeros((8, width - 2 * rank * cap), f32)
        return carry

    lax.fori_loop(0, chunks, one_chunk, 0)


def receive_kernel(target_ref, me_ref, coef_ref, u_ref, *rest):
    outs, accs = rest[:-4], rest[-4:]
    span = len(outs)
    count, cap, rank, width = u_ref.shape[0], u_ref.shape[1], u_ref.shape[3], u_ref.shape[4]
    span_rows = outs[0].shape[1]
    used = 2 * rank * cap
    row_bits = span_rows.bit_length() - 1
    piece = accs[0].shape[0] // span
    peers = 16
    for acc_ref in accs:
        acc_ref[...] = jnp.zeros_like(acc_ref)
    me = me_ref[0]
    lane = lax.broadcasted_iota(jnp.int32, (peers * 8, width), 1)

    def one_chunk(index, carry):
        coef = coef_ref[pl.ds(index * peers, peers)].reshape(peers * 8, width)
        is_im = (lane // rank) % 2 == 1
        real_row = jnp.where(is_im, -coef, coef)
        imag_row = jnp.where(is_im, jnp.roll(coef, rank, 1), jnp.roll(coef, -rank, 1))
        zero = jnp.zeros_like(coef)
        rows = []
        for k in range(cap):
            here = lane // (2 * rank) == k
            rows += [jnp.where(here, real_row, zero), jnp.where(here, imag_row, zero)]
        for i in range(peers):
            peer = index * peers + i
            left = jnp.concatenate([r[8 * i : 8 * i + 8, :used] for r in rows], 0)
            left_high, left_low = split_two(left)
            high, low = split_two(u_ref[peer].reshape(used, width))
            one = jnp.dot(
                jnp.concatenate([left_high, left_low], 0), high, preferred_element_type=f32
            )
            two = jnp.dot(left_high, low, preferred_element_type=f32)
            many = left.shape[0]
            total = one[:many] + (one[many:] + two)
            for k in range(cap):
                w = target_ref[k, peer]
                place = (((w >> row_bits) - me) & (span - 1)) * piece + (w & (span_rows - 1))
                at = pl.ds(place, 16, stride=span_rows)
                acc_ref = accs[(2 * i + k) % 4]
                acc_ref[at, :] += total[16 * k : 16 * k + 16]
        return carry

    lax.fori_loop(0, count // peers, one_chunk, 0)
    for k in range(span):
        at = slice(k * piece, (k + 1) * piece)
        total = (accs[0][at, :] + accs[1][at, :]) + (accs[2][at, :] + accs[3][at, :])
        outs[k][...] = total.reshape(outs[k].shape)


def near_kernel(begin, count, skip, edge, *refs):
    scratch = refs[-8:]
    pos_ref, wide_ref, kern_even, kern_odd, target_ref, source_ref, part_ref, acc_ref = scratch
    if edge:
        left_ref, mid_ref, right_ref, done_ref, field_ref, out_ref = refs[:-8]
    else:
        mid_ref, out_ref, token_ref = refs[:-8]
    blocks = mid_ref.shape[0]
    halo = blocks // 4
    window = 2 * halo + 1
    width = mid_ref.shape[2]
    turn = wavenumber / (2.0 * math.pi)

    def block_in(index):
        if index < halo:
            return left_ref.at[index]
        if index < halo + blocks:
            return mid_ref.at[index - halo]
        return right_ref.at[index - halo - blocks]

    origin = mid_ref[blocks // 2, 16:19, 0:1]
    row = lax.broadcasted_iota(jnp.int32, (8, width), 0)
    for b in range(0 if edge else halo, blocks + (2 if edge else 1) * halo):
        ref = block_in(b)
        pad = jnp.zeros((5, width), f32)
        pos_ref[b, 0:8, :] = jnp.concatenate([(ref[16:19, :] - origin) * turn, pad], 0)
        pos_ref[b, 8:16, :] = jnp.concatenate([ref[19:22, :] * wavenumber, pad], 0)
        re, im = ref[0:8, :], ref[8:16, :]
        rows = jnp.concatenate(
            [jnp.concatenate([re, -im], 1), jnp.concatenate([im, re], 1)], 0
        )
        high, low = split_two(rows)
        wide_ref[:, 2 * width * b : 2 * width * (b + 1)] = jnp.concatenate([high, low], 0)
    sources = window + 1
    zeros = jnp.zeros((width, 2 * width), bf16)
    for kern_ref in (kern_even, kern_odd):
        for part in (0, 2):
            kern_ref[(part + 1) * width : (part + 2) * width, : 2 * width] = zeros
            kern_ref[part * width : (part + 1) * width, 2 * width * (sources - 1) :] = zeros

    chunk = 16
    sub = lax.broadcasted_iota(jnp.int32, (chunk, width), 0)
    lane = lax.broadcasted_iota(jnp.int32, (chunk, width), 1)

    def evaluate(squared, num, at, offset):
        if offset == 0:
            self_pair = (sub + at) == lane
            squared = jnp.where(self_pair, 1.0, squared)
        inv = lax.rsqrt(squared)
        turns = squared * inv
        frac = turns - jnp.round(turns)
        z = frac * frac
        s1 = frac * (SIN_POLY[0] + z * (SIN_POLY[1] + z * SIN_POLY[2]))
        s1_sq = s1 * s1
        c1_sq = 2.0 - s1_sq
        s2 = s1 * (c1_sq * lax.rsqrt(c1_sq))
        c2 = c1_sq - s1_sq
        sine = s2 * c2
        cosine = 1.0 - s2 * (s2 + s2)
        if offset == 0:
            inv = jnp.where(self_pair, 0.0, inv)
        if offset == -halo:
            inv = jnp.where(lane % SEG >= sub % SEG, inv, 0.0)
        if offset == halo:
            inv = jnp.where(lane % SEG <= sub % SEG, inv, 0.0)
        slant = num * inv
        first = (slant * (turn / wavenumber)) * inv
        second = slant + coupling
        pc, ps = inv * cosine, inv * sine
        return first * pc + second * ps, first * ps - second * pc

    def pair_of(step):
        return jnp.where(step < count, step, step + skip) + begin

    def prepare(step, carry):
        tp = pair_of(step)
        center = pos_ref[2 * tp + halo, 0:8, 8 * SEG - 1 : 8 * SEG]

        def local_of(index):
            place = pos_ref[2 * tp + index, 0:8, :] - center
            return place, jnp.sum(place * place, axis=0, keepdims=True)

        for t in range(2):
            place, norm = local_of(halo + t)
            high, mid, low = split_three(
                jnp.where(row < 3, place, jnp.where(row == 3, 1.0, jnp.where(row == 4, norm, 0.0)))
            )
            rows = jnp.transpose(jnp.concatenate([high, high, mid, high, mid, low], 0))
            target_ref[step, t * width : (t + 1) * width, :] = rows.astype(bf16)
        for sb in range(sources):
            place, norm = local_of(sb)
            normal = pos_ref[2 * tp + sb, 8:16, :]
            along = jnp.sum(normal * place, axis=0, keepdims=True)
            wide = []
            for rows in (
                jnp.where(
                    row < 3, -2.0 * place, jnp.where(row == 3, norm, jnp.where(row == 4, 1.0, 0.0))
                ),
                jnp.where(row < 3, normal, jnp.where(row == 3, -along, 0.0)),
            ):
                high, mid, low = split_three(rows)
                wide.append(jnp.concatenate([high, mid, high, low, mid, high], 0))
            cols = slice(2 * width * sb, 2 * width * (sb + 1))
            source_ref[step, :, cols] = jnp.concatenate(wide, 1).astype(bf16)
        return carry

    def pair_kernels(step, kern_ref, finish):
        for sb in range(sources):
            if sb == 3:
                finish()
            if sb == sources - 2:
                part_ref[...] = partial_sums(step, kern_ref, 0)
            start = width if sb == sources - 1 else 0
            stop = width if sb == 0 else 2 * width
            gram = jnp.dot(
                target_ref[step, start:stop, :],
                source_ref[step, :, 2 * width * sb : 2 * width * (sb + 1)],
                preferred_element_type=f32,
            )
            for at in range(start, stop, chunk):
                t = at // width
                part = gram[at - start : at - start + chunk]
                kern = evaluate(part[:, :width], part[:, width:], at % width, sb - halo - t)
                for value, shift in zip(kern, (0, width)):
                    high, low = split_two(value)
                    cols = slice(2 * width * sb + shift, 2 * width * sb + shift + width)
                    kern_ref[at : at + chunk, cols] = high
                    kern_ref[2 * width + at : 2 * width + at + chunk, cols] = low

    def partial_sums(step, kern_ref, half):
        size = width * sources
        start = pl.multiple_of(pair_of(step) * (4 * width) + half * size, 2 * width)
        cols = slice(half * size, (half + 1) * size)
        prod = dot_nt(kern_ref[:, cols], wide_ref[:, pl.ds(start, size)])
        return prod[: 2 * width] + prod[2 * width :]

    def pair_sums(step, slot, kern_ref):
        prod = part_ref[...] + partial_sums(step, kern_ref, 1)
        for t in range(2):
            half = jnp.transpose(prod[t * width : (t + 1) * width])
            acc_ref[:, pl.ds(2 * slot + t, 1), :] = (half[:16] + half[16:])[:, None, :]

    pairs = 2 * count if edge else count
    spare = acc_ref.shape[1] // 2 - 1

    def slot_of(step):
        return pair_of(step) if edge else step

    def two_pairs(index, carry):
        last = jnp.maximum(2 * index - 1, 0)
        slot = jnp.where(index == 0, spare, slot_of(last))
        even = 2 * index
        pair_kernels(even, kern_even, lambda: pair_sums(last, slot, kern_odd))
        pair_kernels(even + 1, kern_odd, lambda: pair_sums(even, slot_of(even), kern_even))
        return carry

    part_ref[...] = jnp.zeros_like(part_ref)
    lax.fori_loop(0, pairs, prepare, 0)
    lax.fori_loop(0, pairs // 2, two_pairs, 0)
    pair_sums(pairs - 1, slot_of(pairs - 1), kern_odd)
    if edge:
        acc_ref[:, 2 * count : 2 * (count + skip), :] = done_ref[...]
        swapped = segment_swap(acc_ref[:, :blocks, :])
        rhs_count = field_ref.shape[1]
        for c in range(2):
            for u in range(rhs_count):
                out_ref[c, u] = swapped[c * rhs_count + u] + 0.5 * field_ref[c, u]
    else:
        out_ref[...] = acc_ref[:, : 2 * pairs, :]
        token_ref[...] = jnp.zeros_like(token_ref)


def vmem(count=1):
    return [pl.BlockSpec(memory_space=pltpu.VMEM)] * count


def smem(count=1):
    return [pl.BlockSpec(memory_space=pltpu.SMEM)] * count


def cost(flops, size):
    return pl.CostEstimate(flops=flops, bytes_accessed=size, transcendentals=0)


def params(megabytes):
    return pltpu.CompilerParams(vmem_limit_bytes=megabytes * 1024 * 1024)


def run_send(chosen, counts, field, positions, normals, areas, v):
    peers, cap, _, rank, width = v.shape
    rhs, span_rows = field.shape[1:3]
    chunks = 4
    blocks = width // SEG
    halo = blocks // 4
    shapes = [(peers, 8, width), (blocks, 24, width), (halo, 24, width), (halo, 24, width)]
    return pl.pallas_call(
        send_kernel,
        in_specs=smem(2) + vmem(4) + [pl.BlockSpec(memory_space=pl.ANY)],
        out_specs=vmem(4),
        out_shape=[jax.ShapeDtypeStruct(s, f32) for s in shapes],
        scratch_shapes=[
            pltpu.VMEM(v.shape, f32),
            pltpu.VMEM((span_rows, 16, 2 * width), bf16),
            pltpu.SemaphoreType.DMA((chunks,)),
        ],
        cost_estimate=cost(3 * 10**9, 4 * v.size),
        compiler_params=params(58),
        name="send",
    )(chosen, counts, field.reshape(2 * rhs * span_rows, width), positions, normals, areas, v)


def run_receive(targets, me, coef, u, span, span_rows):
    width = u.shape[4]
    shape = (16, span_rows, width)
    return pl.pallas_call(
        receive_kernel,
        in_specs=smem(2) + vmem(2),
        out_specs=vmem(span),
        out_shape=[jax.ShapeDtypeStruct(shape, f32)] * span,
        scratch_shapes=[pltpu.VMEM((span * 16 * span_rows, width), f32)] * 4,
        cost_estimate=cost(3 * 10**9, 4 * u.size),
        compiler_params=params(12),
        name="receive",
    )(targets, me, coef, u)


def near_scratch(blocks, width, pairs, slots):
    halo = blocks // 4
    count = blocks + 2 * halo
    span = 2 * width * (2 * halo + 2)
    return [
        pltpu.VMEM((count, 16, width), f32),
        pltpu.VMEM((32, 2 * width * count), bf16),
        pltpu.VMEM((4 * width, span), bf16),
        pltpu.VMEM((4 * width, span), bf16),
        pltpu.VMEM((pairs, 2 * width, 48), bf16),
        pltpu.VMEM((pairs, 48, span), bf16),
        pltpu.VMEM((2 * width, 32), f32),
        pltpu.VMEM((16, 2 * slots + 2, width), f32),
    ]


def run_near_inner(mid):
    blocks, _, width = mid.shape
    halo = blocks // 4
    count = blocks - 2 * halo
    return pl.pallas_call(
        functools.partial(near_kernel, halo // 2, count // 2, 0, False),
        in_specs=vmem(1),
        out_specs=vmem(2),
        out_shape=[
            jax.ShapeDtypeStruct((16, count, width), f32),
            jax.ShapeDtypeStruct((8, width), f32),
        ],
        scratch_shapes=near_scratch(blocks, width, count // 2, count // 2),
        compiler_params=params(20),
        cost_estimate=cost(10**10, 10**6),
        name="near_inner",
    )(mid)


def run_near_edge(left, mid, right, done, field):
    blocks, _, width = mid.shape
    halo = left.shape[0]
    return pl.pallas_call(
        functools.partial(near_kernel, 0, halo // 2, blocks // 2 - halo, True),
        in_specs=vmem(5),
        out_specs=vmem()[0],
        out_shape=jax.ShapeDtypeStruct(field.shape, f32),
        scratch_shapes=near_scratch(blocks, width, halo, blocks // 2),
        compiler_params=params(20),
        cost_estimate=cost(10**10, 10**6),
        name="near_edge",
    )(left, mid, right, done, field)


def shards(
    field, positions, normals, areas, col_cluster, block_count, row_cluster, v_factors, u_factors
):
    azim = lax.axis_size("azim")
    span = lax.axis_size("span")
    span_rows = field.shape[2]
    hold = lax.optimization_barrier
    outgoing, mid, low, high = run_send(
        col_cluster[0, 0].T,
        block_count[0],
        field,
        positions,
        normals,
        areas,
        v_factors.reshape(v_factors.shape[2:]),
    )
    incoming = lax.all_to_all(outgoing, "azim", split_axis=0, concat_axis=0, tiled=True)
    forward = [(i, (i + 1) % azim) for i in range(azim)]
    backward = [(b, a) for a, b in forward]
    left = lax.ppermute(high, "azim", forward)
    right = lax.ppermute(low, "azim", backward)
    inner, token = run_near_inner(mid)
    incoming, _ = hold((incoming, token))
    me = lax.axis_index("span").astype(jnp.int32).reshape(1)
    pieces = run_receive(
        row_cluster[0, 0].T, me, incoming, u_factors.reshape(u_factors.shape[2:]), span, span_rows
    )
    mid, *pieces = hold((mid, *pieces))
    total = pieces[0]
    others = []
    for k in range(1, span):
        ring = [(i, (i + k) % span) for i in range(span)]
        others.append(lax.ppermute(pieces[k], "span", ring))
    near = run_near_edge(left, mid, right, inner, field)
    for other in others:
        total = total + other
    return near + total.reshape(near.shape)


def solution(mesh):
    placed = (
        P(None, None, "span", "azim"),
        P(None, "span", "azim"),
        P(None, "span", "azim"),
        P("span", "azim"),
        P("azim", "span", None, None),
        P("azim", "span", None),
        P("azim", "span", None, None),
        P("azim", "span", None, None, None, None, None),
        P("azim", "span", None, None, None, None, None),
    )
    return jax.shard_map(
        shards, mesh=mesh, in_specs=placed, out_specs=P(None, None, "span", "azim"), check_vma=False
    )
```

```python
import functools
import math

import jax
import jax.numpy as jnp
from jax import lax
from jax.experimental import pallas as pl
from jax.experimental.pallas import tpu as pltpu
from jax.sharding import PartitionSpec as P

wavenumber = 0.9
coupling = 1.1
f32 = jnp.float32
bf16 = jnp.bfloat16

SEG = 8
SIN_POLY = (2.2214303951, -0.9131751650, 0.1098397679)


def split_two(value):
    high = value.astype(bf16)
    return high, (value - high.astype(f32)).astype(bf16)


def split_three(value):
    high = value.astype(bf16).astype(f32)
    rest = value - high
    middle = rest.astype(bf16).astype(f32)
    return high, middle, rest - middle


def dot_nt(left, right):
    return lax.dot_general(left, right, (((1,), (1,)), ((), ())), preferred_element_type=f32)


def segment_swap(value):
    rows = value.shape[1]
    row = lax.broadcasted_iota(jnp.int32, value.shape, 1)
    seg = lax.broadcasted_iota(jnp.int32, value.shape, 2) // SEG
    bit = 1
    while bit < rows:
        row_bit = (row // bit) % 2
        seg_bit = (seg // bit) % 2
        up = jnp.roll(jnp.roll(value, -bit, 1), SEG * bit, 2)
        down = jnp.roll(jnp.roll(value, bit, 1), -SEG * bit, 2)
        value = jnp.where(row_bit == seg_bit, value, jnp.where(row_bit == 0, up, down))
        bit *= 2
    return value


def pack(field_ref, pos_ref, nrm_ref, area_ref, out_ref, low_ref, high_ref):
    span_rows, width = area_ref.shape
    weight = area_ref[...] * (wavenumber / (2.0 * math.pi) / (4.0 * math.pi))
    field = field_ref[...].reshape(field_ref.shape[0] // span_rows, span_rows, width)
    parts = [field[q] * weight for q in range(field.shape[0])]
    parts += [pos_ref[i] for i in range(3)] + [nrm_ref[i] for i in range(3)]
    packed = segment_swap(jnp.stack(parts, 0))
    blocks = out_ref.shape[0]
    for q in range(len(parts)):
        out_ref[:, q, :] = packed[q]
        low_ref[:, q, :] = packed[q, : low_ref.shape[0]]
        high_ref[:, q, :] = packed[q, blocks - high_ref.shape[0] :]


def send_kernel(me_ref, chosen_ref, count_ref, field_ref, pos_ref, nrm_ref, area_ref, v_hbm, *rest):
    outs, (mid_ref, low_ref, high_ref, out_ref, v_ref, table_ref, sems) = rest[:-7], rest[-7:]
    me = me_ref[0]
    chunks = sems.shape[0]
    peers = out_ref.shape[0] // chunks
    rank = v_ref.shape[3]
    cap = v_ref.shape[1]
    width = out_ref.shape[2]
    span_rows = table_ref.shape[0]

    def fetch(index):
        rows = pl.ds(index * peers, peers)
        return pltpu.make_async_copy(v_hbm.at[rows], v_ref.at[rows], sems.at[index])

    ahead = me // peers
    for index in range(chunks):
        fetch(index ^ ahead).start()
    pack(field_ref, pos_ref, nrm_ref, area_ref, mid_ref, low_ref, high_ref)

    half = field_ref.shape[0] // 2
    for row in range(span_rows):
        pair = jnp.concatenate(
            [field_ref[pl.ds(c * half + row, 8, stride=span_rows), :] for c in range(2)], 1
        )
        high, low = split_two(pair)
        table_ref[row] = jnp.concatenate([high.astype(f32), low.astype(f32)], 0).astype(bf16)

    lane = lax.broadcasted_iota(jnp.int32, (8, 2 * rank * cap), 1)

    def one_chunk(index, carry):
        fetch(index ^ ahead).wait()
        for i in range(peers):
            tile = index * peers + i
            peer = tile ^ me
            wide = []
            for k in range(cap):
                re, im = v_ref[peer, k, 0], v_ref[peer, k, 1]
                wide += [jnp.concatenate([re, -im], 1), jnp.concatenate([im, re], 1)]
            high, low = split_two(jnp.concatenate(wide, 0))
            left = jnp.concatenate([table_ref[chosen_ref[k, peer]] for k in range(cap)], 0)
            first = dot_nt(left, high)
            second = dot_nt(left, low)
            total = jnp.zeros((8, 2 * rank * cap), f32)
            for k in range(cap):
                at = 16 * k
                part = first[at : at + 8] + (first[at + 8 : at + 16] + second[at : at + 8])
                here = (lane // (2 * rank) == k) & (k < count_ref[0, peer])
                total = jnp.where(here, part, total)
            out_ref[tile, :, : 2 * rank * cap] = total
            out_ref[tile, :, 2 * rank * cap :] = jnp.zeros((8, width - 2 * rank * cap), f32)
        return carry

    lax.fori_loop(0, chunks, one_chunk, 0)
    for k, ref in enumerate(outs):
        ref[...] = out_ref[k * peers : (k + 1) * peers]


def receive_kernel(target_ref, me_ref, *rest):
    parts, u_ref, outs, coef_ref, accs = rest[:4], rest[4], rest[5:-5], rest[-5], rest[-4:]
    span = len(outs)
    count, cap, rank, width = u_ref.shape[0], u_ref.shape[1], u_ref.shape[3], u_ref.shape[4]
    span_rows = outs[0].shape[1]
    used = 2 * rank * cap
    row_bits = span_rows.bit_length() - 1
    piece = accs[0].shape[0] // span
    peers = 16
    for acc_ref in accs:
        acc_ref[...] = jnp.zeros_like(acc_ref)
    for k, ref in enumerate(parts):
        coef_ref[k * peers : (k + 1) * peers] = ref[...]
    me, sector = me_ref[0], me_ref[1]
    lane = lax.broadcasted_iota(jnp.int32, (peers * 8, width), 1)

    def one_chunk(index, carry):
        coef = coef_ref[pl.ds(index * peers, peers)].reshape(peers * 8, width)
        is_im = (lane // rank) % 2 == 1
        real_row = jnp.where(is_im, -coef, coef)
        imag_row = jnp.where(is_im, jnp.roll(coef, rank, 1), jnp.roll(coef, -rank, 1))
        zero = jnp.zeros_like(coef)
        rows = []
        for k in range(cap):
            here = lane // (2 * rank) == k
            rows += [jnp.where(here, real_row, zero), jnp.where(here, imag_row, zero)]
        for i in range(peers):
            peer = ((i % 4) * 16 + (i // 4) * 4 + index) ^ sector
            left = jnp.concatenate([r[8 * i : 8 * i + 8, :used] for r in rows], 0)
            left_high, left_low = split_two(left)
            high, low = split_two(u_ref[peer].reshape(used, width))
            one = jnp.dot(
                jnp.concatenate([left_high, left_low], 0), high, preferred_element_type=f32
            )
            two = jnp.dot(left_high, low, preferred_element_type=f32)
            many = left.shape[0]
            total = one[:many] + (one[many:] + two)
            for k in range(cap):
                w = target_ref[k, peer]
                place = (((w >> row_bits) - me) & (span - 1)) * piece + (w & (span_rows - 1))
                at = pl.ds(place, 16, stride=span_rows)
                acc_ref = accs[(2 * i + k) % 4]
                acc_ref[at, :] += total[16 * k : 16 * k + 16]
        return carry

    lax.fori_loop(0, count // peers, one_chunk, 0)
    for k in range(span):
        at = slice(k * piece, (k + 1) * piece)
        total = (accs[0][at, :] + accs[1][at, :]) + (accs[2][at, :] + accs[3][at, :])
        outs[k][...] = total.reshape(outs[k].shape)


def near_kernel(begin, final, *refs):
    scratch = refs[-7:]
    pos_ref, wide_ref, kern_ref, target_ref, source_ref, part_ref, acc_ref = scratch
    if final:
        left_ref, mid_ref, right_ref, *done, field_ref, out_ref = refs[:-7]
    else:
        left_ref, mid_ref, right_ref, out_ref, token_ref = refs[:-7]
    pairs = target_ref.shape[0]
    blocks = mid_ref.shape[0]
    halo = blocks // 4
    window = 2 * halo + 1
    width = mid_ref.shape[2]
    turn = wavenumber / (2.0 * math.pi)

    def block_in(local):
        index = 2 * begin - halo + local
        if index < 0:
            return left_ref.at[index + halo]
        if index < blocks:
            return mid_ref.at[index]
        return right_ref.at[index - blocks]

    origin = mid_ref[blocks // 2, 16:19, 0:1]
    row = lax.broadcasted_iota(jnp.int32, (8, width), 0)
    for b in range(pos_ref.shape[0]):
        ref = block_in(b)
        pad = jnp.zeros((5, width), f32)
        pos_ref[b, 0:8, :] = jnp.concatenate([(ref[16:19, :] - origin) * turn, pad], 0)
        pos_ref[b, 8:16, :] = jnp.concatenate([ref[19:22, :] * wavenumber, pad], 0)
        re, im = ref[0:8, :], ref[8:16, :]
        rows = jnp.concatenate(
            [jnp.concatenate([re, -im], 1), jnp.concatenate([im, re], 1)], 0
        )
        high, low = split_two(rows)
        wide_ref[:, 2 * width * b : 2 * width * (b + 1)] = jnp.concatenate([high, low], 0)
    sources = window + 1
    zeros = jnp.zeros((width, 2 * width), bf16)
    for part in (0, 2):
        kern_ref[(part + 1) * width : (part + 2) * width, : 2 * width] = zeros
        kern_ref[part * width : (part + 1) * width, 2 * width * (sources - 1) :] = zeros

    chunk = 16
    sub = lax.broadcasted_iota(jnp.int32, (chunk, width), 0)
    lane = lax.broadcasted_iota(jnp.int32, (chunk, width), 1)

    def evaluate(squared, num, at, offset):
        if offset == 0:
            self_pair = (sub + at) == lane
            squared = jnp.where(self_pair, 1.0, squared)
        inv = lax.rsqrt(squared)
        turns = squared * inv
        frac = turns - jnp.round(turns)
        z = frac * frac
        s1 = frac * (SIN_POLY[0] + z * (SIN_POLY[1] + z * SIN_POLY[2]))
        s1_sq = s1 * s1
        c1_sq = 2.0 - s1_sq
        s2 = s1 * (c1_sq * lax.rsqrt(c1_sq))
        c2 = c1_sq - s1_sq
        sine = s2 * c2
        cosine = 1.0 - s2 * (s2 + s2)
        if offset == 0:
            inv = jnp.where(self_pair, 0.0, inv)
        if offset == -halo:
            inv = jnp.where(lane % SEG >= sub % SEG, inv, 0.0)
        if offset == halo:
            inv = jnp.where(lane % SEG <= sub % SEG, inv, 0.0)
        slant = num * inv
        first = (slant * (turn / wavenumber)) * inv
        second = slant + coupling
        pc, ps = inv * cosine, inv * sine
        return first * pc + second * ps, first * ps - second * pc

    def prepare(step, carry):
        tp = step
        center = pos_ref[2 * tp + halo, 0:8, 8 * SEG - 1 : 8 * SEG]

        def local_of(index):
            place = pos_ref[2 * tp + index, 0:8, :] - center
            return place, jnp.sum(place * place, axis=0, keepdims=True)

        for t in range(2):
            place, norm = local_of(halo + t)
            high, mid, low = split_three(
                jnp.where(row < 3, place, jnp.where(row == 3, 1.0, jnp.where(row == 4, norm, 0.0)))
            )
            rows = jnp.transpose(jnp.concatenate([high, high, mid, high, mid, low], 0))
            target_ref[step, t * width : (t + 1) * width, :] = rows.astype(bf16)
        for sb in range(sources):
            place, norm = local_of(sb)
            normal = pos_ref[2 * tp + sb, 8:16, :]
            along = jnp.sum(normal * place, axis=0, keepdims=True)
            wide = []
            for rows in (
                jnp.where(
                    row < 3, -2.0 * place, jnp.where(row == 3, norm, jnp.where(row == 4, 1.0, 0.0))
                ),
                jnp.where(row < 3, normal, jnp.where(row == 3, -along, 0.0)),
            ):
                high, mid, low = split_three(rows)
                wide.append(jnp.concatenate([high, mid, high, low, mid, high], 0))
            cols = slice(2 * width * sb, 2 * width * (sb + 1))
            source_ref[step, :, cols] = jnp.concatenate(wide, 1).astype(bf16)
        return carry

    def sums(step, index):
        start = pl.multiple_of((2 * step + index) * (2 * width), 2 * width)
        cols = slice(2 * width * index, 2 * width * (index + 1))
        return dot_nt(wide_ref[:, pl.ds(start, 2 * width)], kern_ref[:, cols])

    def finish(step, slot):
        prod = part_ref[...] + sums(step, sources - 1)
        prod = prod[:, : 2 * width] + prod[:, 2 * width :]
        prod = prod[:16] + prod[16:]
        for t in range(2):
            acc_ref[:, pl.ds(2 * slot + t, 1), :] = prod[:, t * width : (t + 1) * width][:, None, :]

    spare = acc_ref.shape[1] // 2 - 1

    def one_pair(step, carry):
        for sb in range(sources):
            start = width if sb == sources - 1 else 0
            stop = width if sb == 0 else 2 * width
            gram = jnp.dot(
                target_ref[step, start:stop, :],
                source_ref[step, :, 2 * width * sb : 2 * width * (sb + 1)],
                preferred_element_type=f32,
            )
            if sb == 0:
                last = jnp.maximum(step - 1, 0)
                finish(last, jnp.where(step == 0, spare, last))
            elif sb == 1:
                part_ref[...] = sums(step, 0)
            else:
                part_ref[...] += sums(step, sb - 1)
            for at in range(start, stop, chunk):
                t = at // width
                part = gram[at - start : at - start + chunk]
                kern = evaluate(part[:, :width], part[:, width:], at % width, sb - halo - t)
                for value, shift in zip(kern, (0, width)):
                    high, low = split_two(value)
                    cols = slice(2 * width * sb + shift, 2 * width * sb + shift + width)
                    kern_ref[at : at + chunk, cols] = high
                    kern_ref[2 * width + at : 2 * width + at + chunk, cols] = low
        return carry

    part_ref[...] = jnp.zeros_like(part_ref)
    lax.fori_loop(0, pairs, prepare, 0)
    lax.fori_loop(0, pairs, one_pair, 0)
    finish(pairs - 1, pairs - 1)
    if final:
        own = 2 * pairs
        for k, ref in enumerate(done):
            acc_ref[:, own * (k + 1) : own * (k + 2), :] = ref[...]
        swapped = segment_swap(acc_ref[:, :blocks, :])
        rhs_count = field_ref.shape[1]
        for c in range(2):
            for u in range(rhs_count):
                out_ref[c, u] = swapped[c * rhs_count + u] + 0.5 * field_ref[c, u]
    else:
        out_ref[...] = acc_ref[:, : 2 * pairs, :]
        token_ref[...] = jnp.zeros_like(token_ref)


def vmem(count=1):
    return [pl.BlockSpec(memory_space=pltpu.VMEM)] * count


def smem(count=1):
    return [pl.BlockSpec(memory_space=pltpu.SMEM)] * count


def cost(flops, size):
    return pl.CostEstimate(flops=flops, bytes_accessed=size, transcendentals=0)


def params(megabytes):
    return pltpu.CompilerParams(vmem_limit_bytes=megabytes * 1024 * 1024)


def run_send(me, chosen, counts, field, positions, normals, areas, v):
    peers, cap, _, rank, width = v.shape
    rhs, span_rows = field.shape[1:3]
    chunks = 4
    blocks = width // SEG
    halo = blocks // 4
    shapes = [(peers // chunks, 8, width)] * chunks
    shapes += [(blocks, 24, width), (halo, 24, width), (halo, 24, width)]
    return pl.pallas_call(
        send_kernel,
        in_specs=smem(3) + vmem(4) + [pl.BlockSpec(memory_space=pl.ANY)],
        out_specs=vmem(len(shapes)),
        out_shape=[jax.ShapeDtypeStruct(s, f32) for s in shapes],
        scratch_shapes=[
            pltpu.VMEM((peers, 8, width), f32),
            pltpu.VMEM(v.shape, f32),
            pltpu.VMEM((span_rows, 16, 2 * width), bf16),
            pltpu.SemaphoreType.DMA((chunks,)),
        ],
        cost_estimate=cost(3 * 10**9, 4 * v.size),
        compiler_params=params(58),
        name="send",
    )(me, chosen, counts, field.reshape(2 * rhs * span_rows, width), positions, normals, areas, v)


def run_receive(targets, where, coefs, u, span, span_rows):
    width = u.shape[4]
    shape = (16, span_rows, width)
    return pl.pallas_call(
        receive_kernel,
        in_specs=smem(2) + vmem(5),
        out_specs=vmem(span),
        out_shape=[jax.ShapeDtypeStruct(shape, f32)] * span,
        scratch_shapes=[pltpu.VMEM((u.shape[0], 8, width), f32)]
        + [pltpu.VMEM((span * 16 * span_rows, width), f32)] * 4,
        cost_estimate=cost(3 * 10**9, 4 * u.size),
        compiler_params=params(12),
        name="receive",
    )(targets, where, *coefs, u)


def run_near(part, left, mid, right, done=(), field=None):
    blocks, _, width = mid.shape
    halo = blocks // 4
    pairs = halo // 2
    sources = 2 * halo + 2
    count = 2 * pairs + 2 * halo
    final = field is not None
    if final:
        out_shape = [jax.ShapeDtypeStruct(field.shape, f32)]
        args = (left, mid, right, *done, field)
    else:
        out_shape = [
            jax.ShapeDtypeStruct((16, 2 * pairs, width), f32),
            jax.ShapeDtypeStruct((8, width), f32),
        ]
        args = (left, mid, right)
    return pl.pallas_call(
        functools.partial(near_kernel, part * pairs, final),
        in_specs=vmem(len(args)),
        out_specs=vmem(len(out_shape)),
        out_shape=out_shape,
        scratch_shapes=[
            pltpu.VMEM((count, 16, width), f32),
            pltpu.VMEM((32, 2 * width * count), bf16),
            pltpu.VMEM((4 * width, 2 * width * sources), bf16),
            pltpu.VMEM((pairs, 2 * width, 48), bf16),
            pltpu.VMEM((pairs, 48, 2 * width * sources), bf16),
            pltpu.VMEM((32, 4 * width), f32),
            pltpu.VMEM((16, (blocks if final else 2 * pairs) + 2, width), f32),
        ],
        cost_estimate=cost(5 * 10**9, 10**6),
        compiler_params=params(12),
        name=f"near_{part}",
    )(*args)


def shards(
    field, positions, normals, areas, col_cluster, block_count, row_cluster, v_factors, u_factors
):
    azim = lax.axis_size("azim")
    span = lax.axis_size("span")
    span_rows = field.shape[2]
    hold = lax.optimization_barrier
    sector = lax.axis_index("azim").astype(jnp.int32)
    me = lax.axis_index("span").astype(jnp.int32)
    *tiles, mid, low, high = run_send(
        sector.reshape(1),
        col_cluster[0, 0].T,
        block_count[0],
        field,
        positions,
        normals,
        areas,
        v_factors.reshape(v_factors.shape[2:]),
    )

    def trade(parts, stride):
        moved = [parts[0]]
        for k in range(1, 4):
            pairs = [(i, i ^ (k * stride)) for i in range(azim)]
            moved.append(lax.ppermute(parts[k], "azim", pairs))
        return moved

    def regroup(parts):
        width = parts[0].shape[0] // 4
        return [
            jnp.concatenate([p[k * width : (k + 1) * width] for p in parts], 0) for k in range(4)
        ]

    tiles = trade(tiles, 16)
    near_1, token = run_near(1, mid, mid, mid)
    tiles, _ = hold((tiles, token))
    tiles, mid, low, high = hold((regroup(tiles), mid, low, high))
    tiles = trade(tiles, 4)
    forward = [(i, (i + 1) % azim) for i in range(azim)]
    backward = [(b, a) for a, b in forward]
    left = lax.ppermute(high, "azim", forward)
    right = lax.ppermute(low, "azim", backward)
    near_2, token = run_near(2, mid, mid, mid)
    tiles, left, right, _ = hold((tiles, left, right, token))
    tiles = [
        jnp.stack([p.reshape(4, 4, *p.shape[1:])[:, k] for p in tiles], 0).reshape(tiles[0].shape)
        for k in range(4)
    ]
    tiles, mid = hold((tiles, mid))
    tiles = trade(tiles, 1)
    near_3, token = run_near(3, left, mid, right)
    tiles, _ = hold((tiles, token))
    pieces = run_receive(
        row_cluster[0, 0].T,
        jnp.stack([me, sector]),
        tiles,
        u_factors.reshape(u_factors.shape[2:]),
        span,
        span_rows,
    )
    mid, *pieces = hold((mid, *pieces))
    total = pieces[0]
    others = []
    for k in range(1, span):
        ring = [(i, (i + k) % span) for i in range(span)]
        others.append(lax.ppermute(pieces[k], "span", ring))
    (near,) = run_near(0, left, mid, right, (near_1, near_2, near_3), field)
    for other in others:
        total = total + other
    return near + total.reshape(near.shape)


def solution(mesh):
    placed = (
        P(None, None, "span", "azim"),
        P(None, "span", "azim"),
        P(None, "span", "azim"),
        P("span", "azim"),
        P("azim", "span", None, None),
        P("azim", "span", None),
        P("azim", "span", None, None),
        P("azim", "span", None, None, None, None, None),
        P("azim", "span", None, None, None, None, None),
    )
    return jax.shard_map(
        shards, mesh=mesh, in_specs=placed, out_specs=P(None, None, "span", "azim"), check_vma=False
    )
```

```python
import functools
import math

import jax
import jax.numpy as jnp
from jax import lax
from jax.experimental import pallas as pl
from jax.experimental.pallas import tpu as pltpu
from jax.sharding import PartitionSpec as P

wavenumber = 0.9
coupling = 1.1
f32 = jnp.float32
bf16 = jnp.bfloat16

SEG = 8
SIN_POLY = (2.2214303951, -0.9131751650, 0.1098397679)


def split_two(value):
    high = value.astype(bf16)
    return high, (value - high.astype(f32)).astype(bf16)


def split_three(value):
    high = value.astype(bf16).astype(f32)
    rest = value - high
    middle = rest.astype(bf16).astype(f32)
    return high, middle, rest - middle


def dot_nt(left, right):
    return lax.dot_general(left, right, (((1,), (1,)), ((), ())), preferred_element_type=f32)


def segment_swap(value):
    rows = value.shape[1]
    row = lax.broadcasted_iota(jnp.int32, value.shape, 1)
    seg = lax.broadcasted_iota(jnp.int32, value.shape, 2) // SEG
    bit = 1
    while bit < rows:
        row_bit = (row // bit) % 2
        seg_bit = (seg // bit) % 2
        up = jnp.roll(jnp.roll(value, -bit, 1), SEG * bit, 2)
        down = jnp.roll(jnp.roll(value, bit, 1), -SEG * bit, 2)
        value = jnp.where(row_bit == seg_bit, value, jnp.where(row_bit == 0, up, down))
        bit *= 2
    return value


def pack(field_ref, pos_ref, nrm_ref, area_ref, out_ref, low_ref, high_ref):
    span_rows, width = area_ref.shape
    weight = area_ref[...] * (wavenumber / (2.0 * math.pi) / (4.0 * math.pi))
    field = field_ref[...].reshape(field_ref.shape[0] // span_rows, span_rows, width)
    parts = [field[q] * weight for q in range(field.shape[0])]
    parts += [pos_ref[i] for i in range(3)] + [nrm_ref[i] for i in range(3)]
    packed = segment_swap(jnp.stack(parts, 0))
    blocks = out_ref.shape[0]
    for q in range(len(parts)):
        out_ref[:, q, :] = packed[q]
        low_ref[:, q, :] = packed[q, : low_ref.shape[0]]
        high_ref[:, q, :] = packed[q, blocks - high_ref.shape[0] :]


def send_kernel(chosen_ref, count_ref, field_ref, pos_ref, nrm_ref, area_ref, v_hbm, *rest):
    out_ref, mid_ref, low_ref, high_ref, v_ref, table_ref, sems = rest
    chunks = sems.shape[0]
    peers = out_ref.shape[0] // chunks
    rank = v_ref.shape[3]
    cap = v_ref.shape[1]
    width = out_ref.shape[2]
    span_rows = table_ref.shape[0]

    def fetch(index):
        rows = pl.ds(index * peers, peers)
        return pltpu.make_async_copy(v_hbm.at[rows], v_ref.at[rows], sems.at[index])

    for index in range(chunks):
        fetch(index).start()
    pack(field_ref, pos_ref, nrm_ref, area_ref, mid_ref, low_ref, high_ref)

    half = field_ref.shape[0] // 2
    for row in range(span_rows):
        pair = jnp.concatenate(
            [field_ref[pl.ds(c * half + row, 8, stride=span_rows), :] for c in range(2)], 1
        )
        high, low = split_two(pair)
        table_ref[row] = jnp.concatenate([high.astype(f32), low.astype(f32)], 0).astype(bf16)

    lane = lax.broadcasted_iota(jnp.int32, (8, 2 * rank * cap), 1)

    def one_chunk(index, carry):
        fetch(index).wait()
        for i in range(peers):
            peer = index * peers + i
            wide = []
            for k in range(cap):
                re, im = v_ref[peer, k, 0], v_ref[peer, k, 1]
                wide += [jnp.concatenate([re, -im], 1), jnp.concatenate([im, re], 1)]
            high, low = split_two(jnp.concatenate(wide, 0))
            left = jnp.concatenate([table_ref[chosen_ref[k, peer]] for k in range(cap)], 0)
            first = dot_nt(left, high)
            second = dot_nt(left, low)
            total = jnp.zeros((8, 2 * rank * cap), f32)
            for k in range(cap):
                at = 16 * k
                part = first[at : at + 8] + (first[at + 8 : at + 16] + second[at : at + 8])
                here = (lane // (2 * rank) == k) & (k < count_ref[0, peer])
                total = jnp.where(here, part, total)
            out_ref[peer, :, : 2 * rank * cap] = total
            out_ref[peer, :, 2 * rank * cap :] = jnp.zeros((8, width - 2 * rank * cap), f32)
        return carry

    lax.fori_loop(0, chunks, one_chunk, 0)


def receive_kernel(target_ref, me_ref, coef_ref, u_ref, *rest):
    outs, accs = rest[:-4], rest[-4:]
    span = len(outs)
    count, cap, rank, width = u_ref.shape[0], u_ref.shape[1], u_ref.shape[3], u_ref.shape[4]
    span_rows = outs[0].shape[1]
    used = 2 * rank * cap
    row_bits = span_rows.bit_length() - 1
    piece = accs[0].shape[0] // span
    peers = 16
    for acc_ref in accs:
        acc_ref[...] = jnp.zeros_like(acc_ref)
    me = me_ref[0]
    lane = lax.broadcasted_iota(jnp.int32, (peers * 8, width), 1)

    def one_chunk(index, carry):
        coef = coef_ref[pl.ds(index * peers, peers)].reshape(peers * 8, width)
        is_im = (lane // rank) % 2 == 1
        real_row = jnp.where(is_im, -coef, coef)
        imag_row = jnp.where(is_im, jnp.roll(coef, rank, 1), jnp.roll(coef, -rank, 1))
        zero = jnp.zeros_like(coef)
        rows = []
        for k in range(cap):
            here = lane // (2 * rank) == k
            rows += [jnp.where(here, real_row, zero), jnp.where(here, imag_row, zero)]
        for i in range(peers):
            peer = index * peers + i
            left = jnp.concatenate([r[8 * i : 8 * i + 8, :used] for r in rows], 0)
            left_high, left_low = split_two(left)
            high, low = split_two(u_ref[peer].reshape(used, width))
            one = jnp.dot(
                jnp.concatenate([left_high, left_low], 0), high, preferred_element_type=f32
            )
            two = jnp.dot(left_high, low, preferred_element_type=f32)
            many = left.shape[0]
            total = one[:many] + (one[many:] + two)
            for k in range(cap):
                w = target_ref[k, peer]
                place = (((w >> row_bits) - me) & (span - 1)) * piece + (w & (span_rows - 1))
                at = pl.ds(place, 16, stride=span_rows)
                acc_ref = accs[(2 * i + k) % 4]
                acc_ref[at, :] += total[16 * k : 16 * k + 16]
        return carry

    lax.fori_loop(0, count // peers, one_chunk, 0)
    for k in range(span):
        at = slice(k * piece, (k + 1) * piece)
        total = (accs[0][at, :] + accs[1][at, :]) + (accs[2][at, :] + accs[3][at, :])
        outs[k][...] = total.reshape(outs[k].shape)


def near_kernel(begin, count, skip, edge, *refs):
    scratch = refs[-7:]
    pos_ref, wide_ref, kern_ref, target_ref, source_ref, part_ref, acc_ref = scratch
    if edge:
        left_ref, mid_ref, right_ref, done_ref, field_ref, out_ref = refs[:-7]
    else:
        mid_ref, out_ref, token_ref = refs[:-7]
    blocks = mid_ref.shape[0]
    halo = blocks // 4
    window = 2 * halo + 1
    width = mid_ref.shape[2]
    turn = wavenumber / (2.0 * math.pi)

    def block_in(index):
        if index < halo:
            return left_ref.at[index]
        if index < halo + blocks:
            return mid_ref.at[index - halo]
        return right_ref.at[index - halo - blocks]

    origin = mid_ref[blocks // 2, 16:19, 0:1]
    row = lax.broadcasted_iota(jnp.int32, (8, width), 0)
    for b in range(0 if edge else halo, blocks + (2 if edge else 1) * halo):
        ref = block_in(b)
        pad = jnp.zeros((5, width), f32)
        pos_ref[b, 0:8, :] = jnp.concatenate([(ref[16:19, :] - origin) * turn, pad], 0)
        pos_ref[b, 8:16, :] = jnp.concatenate([ref[19:22, :] * wavenumber, pad], 0)
        re, im = ref[0:8, :], ref[8:16, :]
        rows = jnp.concatenate(
            [jnp.concatenate([re, -im], 1), jnp.concatenate([im, re], 1)], 0
        )
        high, low = split_two(rows)
        wide_ref[:, 2 * width * b : 2 * width * (b + 1)] = jnp.concatenate([high, low], 0).astype(f32)
    sources = window + 1
    zeros = jnp.zeros((width, 2 * width), f32)
    for part in (0, 2):
        kern_ref[(part + 1) * width : (part + 2) * width, : 2 * width] = zeros
        kern_ref[part * width : (part + 1) * width, 2 * width * (sources - 1) :] = zeros

    chunk = 16
    sub = lax.broadcasted_iota(jnp.int32, (chunk, width), 0)
    lane = lax.broadcasted_iota(jnp.int32, (chunk, width), 1)

    def evaluate(squared, num, at, offset):
        if offset == 0:
            self_pair = (sub + at) == lane
            squared = jnp.where(self_pair, 1.0, squared)
        inv = lax.rsqrt(squared)
        turns = squared * inv
        frac = turns - jnp.round(turns)
        z = frac * frac
        s1 = frac * (SIN_POLY[0] + z * (SIN_POLY[1] + z * SIN_POLY[2]))
        s1_sq = s1 * s1
        c1_sq = 2.0 - s1_sq
        s2 = s1 * (c1_sq * lax.rsqrt(c1_sq))
        c2 = c1_sq - s1_sq
        sine = s2 * c2
        cosine = 1.0 - s2 * (s2 + s2)
        if offset == 0:
            inv = jnp.where(self_pair, 0.0, inv)
        if offset == -halo:
            inv = jnp.where(lane % SEG >= sub % SEG, inv, 0.0)
        if offset == halo:
            inv = jnp.where(lane % SEG <= sub % SEG, inv, 0.0)
        slant = num * inv
        first = (slant * (turn / wavenumber)) * inv
        second = slant + coupling
        pc, ps = inv * cosine, inv * sine
        return first * pc + second * ps, first * ps - second * pc

    def pair_of(step):
        return jnp.where(step < count, step, step + skip) + begin

    def prepare(step, carry):
        tp = pair_of(step)
        center = pos_ref[2 * tp + halo, 0:8, 8 * SEG - 1 : 8 * SEG]

        def local_of(index):
            place = pos_ref[2 * tp + index, 0:8, :] - center
            return place, jnp.sum(place * place, axis=0, keepdims=True)

        for t in range(2):
            place, norm = local_of(halo + t)
            high, mid, low = split_three(
                jnp.where(row < 3, place, jnp.where(row == 3, 1.0, jnp.where(row == 4, norm, 0.0)))
            )
            rows = jnp.transpose(jnp.concatenate([high, high, mid, high, mid, low], 0))
            target_ref[step, t * width : (t + 1) * width, :] = rows.astype(bf16)
        for sb in range(sources):
            place, norm = local_of(sb)
            normal = pos_ref[2 * tp + sb, 8:16, :]
            along = jnp.sum(normal * place, axis=0, keepdims=True)
            wide = []
            for rows in (
                jnp.where(
                    row < 3, -2.0 * place, jnp.where(row == 3, norm, jnp.where(row == 4, 1.0, 0.0))
                ),
                jnp.where(row < 3, normal, jnp.where(row == 3, -along, 0.0)),
            ):
                high, mid, low = split_three(rows)
                wide.append(jnp.concatenate([high, mid, high, low, mid, high], 0))
            cols = slice(2 * width * sb, 2 * width * (sb + 1))
            source_ref[step, :, cols] = jnp.concatenate(wide, 1).astype(bf16)
        return carry

    batch = 2

    def sums(step, index):
        size = 2 * width * batch
        start = pl.multiple_of(pair_of(step) * (4 * width) + size * index, 2 * width)
        prod = dot_nt(
            kern_ref[:, size * index : size * (index + 1)], wide_ref[:, pl.ds(start, size)]
        )
        return prod[: 2 * width] + prod[2 * width :]

    def finish(step, slot):
        prod = part_ref[...] + sums(step, sources // batch - 1)
        for t in range(2):
            half = jnp.transpose(prod[t * width : (t + 1) * width])
            acc_ref[:, pl.ds(2 * slot + t, 1), :] = (half[:16] + half[16:])[:, None, :]

    pairs = 2 * count if edge else count
    spare = acc_ref.shape[1] // 2 - 1

    def slot_of(step):
        return pair_of(step) if edge else step

    def rows_of(sb):
        return (width if sb == sources - 1 else 0), (width if sb == 0 else 2 * width)

    def gram_of(step, sb):
        start, stop = rows_of(sb)
        return jnp.dot(
            target_ref[step, start:stop, :],
            source_ref[step, :, 2 * width * sb : 2 * width * (sb + 1)],
            preferred_element_type=f32,
        )

    def one_pair(step, carry):
        for sb in range(sources):
            start, stop = rows_of(sb)
            gram = gram_of(step, sb)
            done = sb - 1 if sb % batch == 1 % batch else -1
            if sb == 1:
                last = jnp.maximum(step - 1, 0)
                finish(last, jnp.where(step == 0, spare, slot_of(last)))
            elif sb > batch and done >= 0:
                index = done // batch - 1
                if index == 0:
                    part_ref[...] = sums(step, 0)
                else:
                    part_ref[...] += sums(step, index)
            for at in range(start, stop, chunk):
                t = at // width
                part = gram[at - start : at - start + chunk]
                kern = evaluate(part[:, :width], part[:, width:], at % width, sb - halo - t)
                for value, shift in zip(kern, (0, width)):
                    high, low = value, value - value.astype(bf16).astype(f32)
                    cols = slice(2 * width * sb + shift, 2 * width * sb + shift + width)
                    kern_ref[at : at + chunk, cols] = high
                    kern_ref[2 * width + at : 2 * width + at + chunk, cols] = low
        return carry

    part_ref[...] = jnp.zeros_like(part_ref)
    lax.fori_loop(0, pairs, prepare, 0)
    lax.fori_loop(0, pairs, one_pair, 0)
    finish(pairs - 1, slot_of(pairs - 1))
    if edge:
        acc_ref[:, 2 * count : 2 * (count + skip), :] = done_ref[...]
        swapped = segment_swap(acc_ref[:, :blocks, :])
        rhs_count = field_ref.shape[1]
        for c in range(2):
            for u in range(rhs_count):
                out_ref[c, u] = swapped[c * rhs_count + u] + 0.5 * field_ref[c, u]
    else:
        out_ref[...] = acc_ref[:, : 2 * pairs, :]
        token_ref[...] = jnp.zeros_like(token_ref)


def vmem(count=1):
    return [pl.BlockSpec(memory_space=pltpu.VMEM)] * count


def smem(count=1):
    return [pl.BlockSpec(memory_space=pltpu.SMEM)] * count


def cost(flops, size):
    return pl.CostEstimate(flops=flops, bytes_accessed=size, transcendentals=0)


def params(megabytes):
    return pltpu.CompilerParams(vmem_limit_bytes=megabytes * 1024 * 1024)


def run_send(chosen, counts, field, positions, normals, areas, v):
    peers, cap, _, rank, width = v.shape
    rhs, span_rows = field.shape[1:3]
    chunks = 4
    blocks = width // SEG
    halo = blocks // 4
    shapes = [(peers, 8, width), (blocks, 24, width), (halo, 24, width), (halo, 24, width)]
    return pl.pallas_call(
        send_kernel,
        in_specs=smem(2) + vmem(4) + [pl.BlockSpec(memory_space=pl.ANY)],
        out_specs=vmem(4),
        out_shape=[jax.ShapeDtypeStruct(s, f32) for s in shapes],
        scratch_shapes=[
            pltpu.VMEM(v.shape, f32),
            pltpu.VMEM((span_rows, 16, 2 * width), bf16),
            pltpu.SemaphoreType.DMA((chunks,)),
        ],
        cost_estimate=cost(3 * 10**9, 4 * v.size),
        compiler_params=params(58),
        name="send",
    )(chosen, counts, field.reshape(2 * rhs * span_rows, width), positions, normals, areas, v)


def run_receive(targets, me, coef, u, span, span_rows):
    width = u.shape[4]
    shape = (16, span_rows, width)
    return pl.pallas_call(
        receive_kernel,
        in_specs=smem(2) + vmem(2),
        out_specs=vmem(span),
        out_shape=[jax.ShapeDtypeStruct(shape, f32)] * span,
        scratch_shapes=[pltpu.VMEM((span * 16 * span_rows, width), f32)] * 4,
        cost_estimate=cost(3 * 10**9, 4 * u.size),
        compiler_params=params(12),
        name="receive",
    )(targets, me, coef, u)


def near_scratch(blocks, width, pairs, slots):
    halo = blocks // 4
    count = blocks + 2 * halo
    span = 2 * width * (2 * halo + 2)
    return [
        pltpu.VMEM((count, 16, width), f32),
        pltpu.VMEM((32, 2 * width * count), f32),
        pltpu.VMEM((4 * width, span), f32),
        pltpu.VMEM((pairs, 2 * width, 48), bf16),
        pltpu.VMEM((pairs, 48, span), bf16),
        pltpu.VMEM((2 * width, 32), f32),
        pltpu.VMEM((16, 2 * slots + 2, width), f32),
    ]


def run_near_inner(mid):
    blocks, _, width = mid.shape
    halo = blocks // 4
    count = blocks - 2 * halo
    return pl.pallas_call(
        functools.partial(near_kernel, halo // 2, count // 2, 0, False),
        in_specs=vmem(1),
        out_specs=vmem(2),
        out_shape=[
            jax.ShapeDtypeStruct((16, count, width), f32),
            jax.ShapeDtypeStruct((8, width), f32),
        ],
        scratch_shapes=near_scratch(blocks, width, count // 2, count // 2),
        compiler_params=params(20),
        cost_estimate=cost(10**10, 10**6),
        name="near_inner",
    )(mid)


def run_near_edge(left, mid, right, done, field):
    blocks, _, width = mid.shape
    halo = left.shape[0]
    return pl.pallas_call(
        functools.partial(near_kernel, 0, halo // 2, blocks // 2 - halo, True),
        in_specs=vmem(5),
        out_specs=vmem()[0],
        out_shape=jax.ShapeDtypeStruct(field.shape, f32),
        scratch_shapes=near_scratch(blocks, width, halo, blocks // 2),
        compiler_params=params(20),
        cost_estimate=cost(10**10, 10**6),
        name="near_edge",
    )(left, mid, right, done, field)


def shards(
    field, positions, normals, areas, col_cluster, block_count, row_cluster, v_factors, u_factors
):
    azim = lax.axis_size("azim")
    span = lax.axis_size("span")
    span_rows = field.shape[2]
    hold = lax.optimization_barrier
    outgoing, mid, low, high = run_send(
        col_cluster[0, 0].T,
        block_count[0],
        field,
        positions,
        normals,
        areas,
        v_factors.reshape(v_factors.shape[2:]),
    )
    incoming = lax.all_to_all(outgoing, "azim", split_axis=0, concat_axis=0, tiled=True)
    forward = [(i, (i + 1) % azim) for i in range(azim)]
    backward = [(b, a) for a, b in forward]
    left = lax.ppermute(high, "azim", forward)
    right = lax.ppermute(low, "azim", backward)
    inner, token = run_near_inner(mid)
    incoming, _ = hold((incoming, token))
    me = lax.axis_index("span").astype(jnp.int32).reshape(1)
    pieces = run_receive(
        row_cluster[0, 0].T, me, incoming, u_factors.reshape(u_factors.shape[2:]), span, span_rows
    )
    mid, *pieces = hold((mid, *pieces))
    total = pieces[0]
    others = []
    for k in range(1, span):
        ring = [(i, (i + k) % span) for i in range(span)]
        others.append(lax.ppermute(pieces[k], "span", ring))
    near = run_near_edge(left, mid, right, inner, field)
    for other in others:
        total = total + other
    return near + total.reshape(near.shape)


def solution(mesh):
    placed = (
        P(None, None, "span", "azim"),
        P(None, "span", "azim"),
        P(None, "span", "azim"),
        P("span", "azim"),
        P("azim", "span", None, None),
        P("azim", "span", None),
        P("azim", "span", None, None),
        P("azim", "span", None, None, None, None, None),
        P("azim", "span", None, None, None, None, None),
    )
    return jax.shard_map(
        shards, mesh=mesh, in_specs=placed, out_specs=P(None, None, "span", "azim"), check_vma=False
    )
```

```python
import functools
import math

import jax
import jax.numpy as jnp
from jax import lax
from jax.experimental import pallas as pl
from jax.experimental.pallas import tpu as pltpu
from jax.sharding import PartitionSpec as P

wavenumber = 0.9
coupling = 1.1
f32 = jnp.float32
bf16 = jnp.bfloat16

SEG = 8
SIN_POLY = (2.2214303951, -0.9131751650, 0.1098397679)


def split_two(value):
    high = value.astype(bf16)
    return high, (value - high.astype(f32)).astype(bf16)


def split_three(value):
    high = value.astype(bf16).astype(f32)
    rest = value - high
    middle = rest.astype(bf16).astype(f32)
    return high, middle, rest - middle


def dot_nt(left, right):
    return lax.dot_general(left, right, (((1,), (1,)), ((), ())), preferred_element_type=f32)


def segment_swap(value):
    rows = value.shape[1]
    row = lax.broadcasted_iota(jnp.int32, value.shape, 1)
    seg = lax.broadcasted_iota(jnp.int32, value.shape, 2) // SEG
    bit = 1
    while bit < rows:
        row_bit = (row // bit) % 2
        seg_bit = (seg // bit) % 2
        up = jnp.roll(jnp.roll(value, -bit, 1), SEG * bit, 2)
        down = jnp.roll(jnp.roll(value, bit, 1), -SEG * bit, 2)
        value = jnp.where(row_bit == seg_bit, value, jnp.where(row_bit == 0, up, down))
        bit *= 2
    return value


def pack(field_ref, pos_ref, nrm_ref, area_ref, out_ref, low_ref, high_ref):
    span_rows, width = area_ref.shape
    weight = area_ref[...] * (wavenumber / (2.0 * math.pi) / (4.0 * math.pi))
    field = field_ref[...].reshape(field_ref.shape[0] // span_rows, span_rows, width)
    parts = [field[q] * weight for q in range(field.shape[0])]
    parts += [pos_ref[i] for i in range(3)] + [nrm_ref[i] for i in range(3)]
    packed = segment_swap(jnp.stack(parts, 0))
    blocks = out_ref.shape[0]
    for q in range(len(parts)):
        out_ref[:, q, :] = packed[q]
        low_ref[:, q, :] = packed[q, : low_ref.shape[0]]
        high_ref[:, q, :] = packed[q, blocks - high_ref.shape[0] :]


def send_kernel(chosen_ref, count_ref, field_ref, pos_ref, nrm_ref, area_ref, v_hbm, *rest):
    out_ref, mid_ref, low_ref, high_ref, v_ref, table_ref, sems = rest
    chunks = sems.shape[0]
    peers = out_ref.shape[0] // chunks
    rank = v_ref.shape[3]
    cap = v_ref.shape[1]
    width = out_ref.shape[2]
    span_rows = table_ref.shape[0]

    def fetch(index):
        rows = pl.ds(index * peers, peers)
        return pltpu.make_async_copy(v_hbm.at[rows], v_ref.at[rows], sems.at[index])

    for index in range(chunks):
        fetch(index).start()
    pack(field_ref, pos_ref, nrm_ref, area_ref, mid_ref, low_ref, high_ref)

    half = field_ref.shape[0] // 2
    for row in range(span_rows):
        re, im = (field_ref[pl.ds(c * half + row, 8, stride=span_rows), :] for c in range(2))
        high, low = split_two(
            jnp.concatenate(
                [jnp.concatenate([re, -im], 1), jnp.concatenate([im, re], 1)], 0
            )
        )
        table_ref[row] = jnp.concatenate([high, low], 0)

    def one_chunk(index, carry):
        fetch(index).wait()
        for i in range(peers):
            peer = index * peers + i
            right = jnp.concatenate(
                [jnp.concatenate([v_ref[peer, k, 0], v_ref[peer, k, 1]], 1) for k in range(cap)], 0
            )
            high, low = split_two(right)
            rows = [table_ref[chosen_ref[k, peer]] for k in range(cap)]
            first = dot_nt(jnp.concatenate(rows, 0), high)
            second = dot_nt(jnp.concatenate([r[:16] for r in rows], 0), low)
            tile = []
            for k in range(cap):
                both = first[32 * k : 32 * k + 16] + (
                    first[32 * k + 16 : 32 * k + 32] + second[16 * k : 16 * k + 16]
                )
                both = jnp.where(k < count_ref[0, peer], both, 0.0)
                cols = slice(k * rank, (k + 1) * rank)
                tile += [both[:8, cols], both[8:, cols]]
            tile.append(jnp.zeros((8, width - 2 * rank * cap), f32))
            out_ref[peer] = jnp.concatenate(tile, 1)
        return carry

    lax.fori_loop(0, chunks, one_chunk, 0)


def receive_kernel(target_ref, me_ref, coef_ref, u_ref, *rest):
    outs, accs = rest[:-4], rest[-4:]
    span = len(outs)
    count, cap, rank, width = u_ref.shape[0], u_ref.shape[1], u_ref.shape[3], u_ref.shape[4]
    span_rows = outs[0].shape[1]
    used = 2 * rank * cap
    row_bits = span_rows.bit_length() - 1
    piece = accs[0].shape[0] // span
    peers = 16
    for acc_ref in accs:
        acc_ref[...] = jnp.zeros_like(acc_ref)
    me = me_ref[0]
    lane = lax.broadcasted_iota(jnp.int32, (peers * 8, width), 1)

    def one_chunk(index, carry):
        coef = coef_ref[pl.ds(index * peers, peers)].reshape(peers * 8, width)
        is_im = (lane // rank) % 2 == 1
        real_row = jnp.where(is_im, -coef, coef)
        imag_row = jnp.where(is_im, jnp.roll(coef, rank, 1), jnp.roll(coef, -rank, 1))
        zero = jnp.zeros_like(coef)
        rows = []
        for k in range(cap):
            here = lane // (2 * rank) == k
            rows += [jnp.where(here, real_row, zero), jnp.where(here, imag_row, zero)]
        for i in range(peers):
            peer = index * peers + i
            left = jnp.concatenate([r[8 * i : 8 * i + 8, :used] for r in rows], 0)
            left_high, left_low = split_two(left)
            high, low = split_two(u_ref[peer].reshape(used, width))
            one = jnp.dot(
                jnp.concatenate([left_high, left_low], 0), high, preferred_element_type=f32
            )
            two = jnp.dot(left_high, low, preferred_element_type=f32)
            many = left.shape[0]
            total = one[:many] + (one[many:] + two)
            for k in range(cap):
                w = target_ref[k, peer]
                place = (((w >> row_bits) - me) & (span - 1)) * piece + (w & (span_rows - 1))
                at = pl.ds(place, 16, stride=span_rows)
                acc_ref = accs[(2 * i + k) % 4]
                acc_ref[at, :] += total[16 * k : 16 * k + 16]
        return carry

    lax.fori_loop(0, count // peers, one_chunk, 0)
    for k in range(span):
        at = slice(k * piece, (k + 1) * piece)
        total = (accs[0][at, :] + accs[1][at, :]) + (accs[2][at, :] + accs[3][at, :])
        outs[k][...] = total.reshape(outs[k].shape)


def near_kernel(begin, count, skip, edge, *refs):
    scratch = refs[-7:]
    pos_ref, wide_ref, kern_ref, target_ref, source_ref, part_ref, acc_ref = scratch
    if edge:
        left_ref, mid_ref, right_ref, done_ref, field_ref, out_ref = refs[:-7]
    else:
        mid_ref, out_ref, token_ref = refs[:-7]
    blocks = mid_ref.shape[0]
    halo = blocks // 4
    window = 2 * halo + 1
    width = mid_ref.shape[2]
    turn = wavenumber / (2.0 * math.pi)

    def block_in(index):
        if index < halo:
            return left_ref.at[index]
        if index < halo + blocks:
            return mid_ref.at[index - halo]
        return right_ref.at[index - halo - blocks]

    origin = mid_ref[blocks // 2, 16:19, 0:1]
    row = lax.broadcasted_iota(jnp.int32, (8, width), 0)
    for b in range(0 if edge else halo, blocks + (2 if edge else 1) * halo):
        ref = block_in(b)
        pad = jnp.zeros((5, width), f32)
        pos_ref[b, 0:8, :] = jnp.concatenate([(ref[16:19, :] - origin) * turn, pad], 0)
        pos_ref[b, 8:16, :] = jnp.concatenate([ref[19:22, :] * wavenumber, pad], 0)
        re, im = ref[0:8, :], ref[8:16, :]
        rows = jnp.concatenate(
            [jnp.concatenate([re, -im], 1), jnp.concatenate([im, re], 1)], 0
        )
        high, low = split_two(rows)
        wide_ref[:, 2 * width * b : 2 * width * (b + 1)] = jnp.concatenate([high, low], 0).astype(f32)
    sources = window + 1
    zeros = jnp.zeros((width, 2 * width), f32)
    for part in (0, 2):
        kern_ref[(part + 1) * width : (part + 2) * width, : 2 * width] = zeros
        kern_ref[part * width : (part + 1) * width, 2 * width * (sources - 1) :] = zeros

    chunk = 16
    sub = lax.broadcasted_iota(jnp.int32, (chunk, width), 0)
    lane = lax.broadcasted_iota(jnp.int32, (chunk, width), 1)

    def evaluate(squared, num, at, offset):
        if offset == 0:
            self_pair = (sub + at) == lane
            squared = jnp.where(self_pair, 1.0, squared)
        inv = lax.rsqrt(squared)
        turns = squared * inv
        frac = turns - jnp.round(turns)
        z = frac * frac
        s1 = frac * (SIN_POLY[0] + z * (SIN_POLY[1] + z * SIN_POLY[2]))
        s1_sq = s1 * s1
        c1_sq = 2.0 - s1_sq
        s2 = s1 * (c1_sq * lax.rsqrt(c1_sq))
        c2 = c1_sq - s1_sq
        sine = s2 * c2
        cosine = 1.0 - s2 * (s2 + s2)
        if offset == 0:
            inv = jnp.where(self_pair, 0.0, inv)
        if offset == -halo:
            inv = jnp.where(lane % SEG >= sub % SEG, inv, 0.0)
        if offset == halo:
            inv = jnp.where(lane % SEG <= sub % SEG, inv, 0.0)
        slant = num * inv
        first = (slant * (turn / wavenumber)) * inv
        second = slant + coupling
        pc, ps = inv * cosine, inv * sine
        return first * pc + second * ps, first * ps - second * pc

    def pair_of(step):
        return jnp.where(step < count, step, step + skip) + begin

    def prepare(step, carry):
        tp = pair_of(step)
        center = pos_ref[2 * tp + halo, 0:8, 8 * SEG - 1 : 8 * SEG]

        def local_of(index):
            place = pos_ref[2 * tp + index, 0:8, :] - center
            return place, jnp.sum(place * place, axis=0, keepdims=True)

        for t in range(2):
            place, norm = local_of(halo + t)
            high, mid, low = split_three(
                jnp.where(row < 3, place, jnp.where(row == 3, 1.0, jnp.where(row == 4, norm, 0.0)))
            )
            rows = jnp.transpose(jnp.concatenate([high, high, mid, high, mid, low], 0))
            target_ref[step, t * width : (t + 1) * width, :] = rows.astype(bf16)
        for sb in range(sources):
            place, norm = local_of(sb)
            normal = pos_ref[2 * tp + sb, 8:16, :]
            along = jnp.sum(normal * place, axis=0, keepdims=True)
            wide = []
            for rows in (
                jnp.where(
                    row < 3, -2.0 * place, jnp.where(row == 3, norm, jnp.where(row == 4, 1.0, 0.0))
                ),
                jnp.where(row < 3, normal, jnp.where(row == 3, -along, 0.0)),
            ):
                high, mid, low = split_three(rows)
                wide.append(jnp.concatenate([high, mid, high, low, mid, high], 0))
            cols = slice(2 * width * sb, 2 * width * (sb + 1))
            source_ref[step, :, cols] = jnp.concatenate(wide, 1).astype(bf16)
        return carry

    batch = 2

    def sums(step, index):
        size = 2 * width * batch
        start = pl.multiple_of(pair_of(step) * (4 * width) + size * index, 2 * width)
        prod = dot_nt(
            kern_ref[:, size * index : size * (index + 1)], wide_ref[:, pl.ds(start, size)]
        )
        return prod[: 2 * width] + prod[2 * width :]

    def finish(step, slot):
        prod = part_ref[...] + sums(step, sources // batch - 1)
        for t in range(2):
            half = jnp.transpose(prod[t * width : (t + 1) * width])
            acc_ref[:, pl.ds(2 * slot + t, 1), :] = (half[:16] + half[16:])[:, None, :]

    pairs = 2 * count if edge else count
    spare = acc_ref.shape[1] // 2 - 1

    def slot_of(step):
        return pair_of(step) if edge else step

    def rows_of(sb):
        return (width if sb == sources - 1 else 0), (width if sb == 0 else 2 * width)

    def gram_of(step, sb):
        start, stop = rows_of(sb)
        return jnp.dot(
            target_ref[step, start:stop, :],
            source_ref[step, :, 2 * width * sb : 2 * width * (sb + 1)],
            preferred_element_type=f32,
        )

    def one_pair(step, carry):
        for sb in range(sources):
            start, stop = rows_of(sb)
            gram = gram_of(step, sb)
            done = sb - 1 if sb % batch == 1 % batch else -1
            if sb == 1:
                last = jnp.maximum(step - 1, 0)
                finish(last, jnp.where(step == 0, spare, slot_of(last)))
            elif sb > batch and done >= 0:
                index = done // batch - 1
                if index == 0:
                    part_ref[...] = sums(step, 0)
                else:
                    part_ref[...] += sums(step, index)
            for at in range(start, stop, chunk):
                t = at // width
                part = gram[at - start : at - start + chunk]
                kern = evaluate(part[:, :width], part[:, width:], at % width, sb - halo - t)
                for value, shift in zip(kern, (0, width)):
                    high, low = value, value - value.astype(bf16).astype(f32)
                    cols = slice(2 * width * sb + shift, 2 * width * sb + shift + width)
                    kern_ref[at : at + chunk, cols] = high
                    kern_ref[2 * width + at : 2 * width + at + chunk, cols] = low
        return carry

    part_ref[...] = jnp.zeros_like(part_ref)
    lax.fori_loop(0, pairs, prepare, 0)
    lax.fori_loop(0, pairs, one_pair, 0)
    finish(pairs - 1, slot_of(pairs - 1))
    if edge:
        acc_ref[:, 2 * count : 2 * (count + skip), :] = done_ref[...]
        swapped = segment_swap(acc_ref[:, :blocks, :])
        rhs_count = field_ref.shape[1]
        for c in range(2):
            for u in range(rhs_count):
                out_ref[c, u] = swapped[c * rhs_count + u] + 0.5 * field_ref[c, u]
    else:
        out_ref[...] = acc_ref[:, : 2 * pairs, :]
        token_ref[...] = jnp.zeros_like(token_ref)


def vmem(count=1):
    return [pl.BlockSpec(memory_space=pltpu.VMEM)] * count


def smem(count=1):
    return [pl.BlockSpec(memory_space=pltpu.SMEM)] * count


def cost(flops, size):
    return pl.CostEstimate(flops=flops, bytes_accessed=size, transcendentals=0)


def params(megabytes):
    return pltpu.CompilerParams(vmem_limit_bytes=megabytes * 1024 * 1024)


def run_send(chosen, counts, field, positions, normals, areas, v):
    peers, cap, _, rank, width = v.shape
    rhs, span_rows = field.shape[1:3]
    chunks = 4
    blocks = width // SEG
    halo = blocks // 4
    shapes = [(peers, 8, width), (blocks, 24, width), (halo, 24, width), (halo, 24, width)]
    return pl.pallas_call(
        send_kernel,
        in_specs=smem(2) + vmem(4) + [pl.BlockSpec(memory_space=pl.ANY)],
        out_specs=vmem(4),
        out_shape=[jax.ShapeDtypeStruct(s, f32) for s in shapes],
        scratch_shapes=[
            pltpu.VMEM(v.shape, f32),
            pltpu.VMEM((span_rows, 32, 2 * width), bf16),
            pltpu.SemaphoreType.DMA((chunks,)),
        ],
        cost_estimate=cost(3 * 10**9, 4 * v.size),
        compiler_params=params(58),
        name="send",
    )(chosen, counts, field.reshape(2 * rhs * span_rows, width), positions, normals, areas, v)


def run_receive(targets, me, coef, u, span, span_rows):
    width = u.shape[4]
    shape = (16, span_rows, width)
    return pl.pallas_call(
        receive_kernel,
        in_specs=smem(2) + vmem(2),
        out_specs=vmem(span),
        out_shape=[jax.ShapeDtypeStruct(shape, f32)] * span,
        scratch_shapes=[pltpu.VMEM((span * 16 * span_rows, width), f32)] * 4,
        cost_estimate=cost(3 * 10**9, 4 * u.size),
        compiler_params=params(12),
        name="receive",
    )(targets, me, coef, u)


def near_scratch(blocks, width, pairs, slots):
    halo = blocks // 4
    count = blocks + 2 * halo
    span = 2 * width * (2 * halo + 2)
    return [
        pltpu.VMEM((count, 16, width), f32),
        pltpu.VMEM((32, 2 * width * count), f32),
        pltpu.VMEM((4 * width, span), f32),
        pltpu.VMEM((pairs, 2 * width, 48), bf16),
        pltpu.VMEM((pairs, 48, span), bf16),
        pltpu.VMEM((2 * width, 32), f32),
        pltpu.VMEM((16, 2 * slots + 2, width), f32),
    ]


def run_near_inner(mid):
    blocks, _, width = mid.shape
    halo = blocks // 4
    count = blocks - 2 * halo
    return pl.pallas_call(
        functools.partial(near_kernel, halo // 2, count // 2, 0, False),
        in_specs=vmem(1),
        out_specs=vmem(2),
        out_shape=[
            jax.ShapeDtypeStruct((16, count, width), f32),
            jax.ShapeDtypeStruct((8, width), f32),
        ],
        scratch_shapes=near_scratch(blocks, width, count // 2, count // 2),
        compiler_params=params(20),
        cost_estimate=cost(10**10, 10**6),
        name="near_inner",
    )(mid)


def run_near_edge(left, mid, right, done, field):
    blocks, _, width = mid.shape
    halo = left.shape[0]
    return pl.pallas_call(
        functools.partial(near_kernel, 0, halo // 2, blocks // 2 - halo, True),
        in_specs=vmem(5),
        out_specs=vmem()[0],
        out_shape=jax.ShapeDtypeStruct(field.shape, f32),
        scratch_shapes=near_scratch(blocks, width, halo, blocks // 2),
        compiler_params=params(20),
        cost_estimate=cost(10**10, 10**6),
        name="near_edge",
    )(left, mid, right, done, field)


def shards(
    field, positions, normals, areas, col_cluster, block_count, row_cluster, v_factors, u_factors
):
    azim = lax.axis_size("azim")
    span = lax.axis_size("span")
    span_rows = field.shape[2]
    hold = lax.optimization_barrier
    outgoing, mid, low, high = run_send(
        col_cluster[0, 0].T,
        block_count[0],
        field,
        positions,
        normals,
        areas,
        v_factors.reshape(v_factors.shape[2:]),
    )
    incoming = lax.all_to_all(outgoing, "azim", split_axis=0, concat_axis=0, tiled=True)
    forward = [(i, (i + 1) % azim) for i in range(azim)]
    backward = [(b, a) for a, b in forward]
    left = lax.ppermute(high, "azim", forward)
    right = lax.ppermute(low, "azim", backward)
    inner, token = run_near_inner(mid)
    incoming, _ = hold((incoming, token))
    me = lax.axis_index("span").astype(jnp.int32).reshape(1)
    pieces = run_receive(
        row_cluster[0, 0].T, me, incoming, u_factors.reshape(u_factors.shape[2:]), span, span_rows
    )
    mid, *pieces = hold((mid, *pieces))
    total = pieces[0]
    others = []
    for k in range(1, span):
        ring = [(i, (i + k) % span) for i in range(span)]
        others.append(lax.ppermute(pieces[k], "span", ring))
    near = run_near_edge(left, mid, right, inner, field)
    for other in others:
        total = total + other
    return near + total.reshape(near.shape)


def solution(mesh):
    placed = (
        P(None, None, "span", "azim"),
        P(None, "span", "azim"),
        P(None, "span", "azim"),
        P("span", "azim"),
        P("azim", "span", None, None),
        P("azim", "span", None),
        P("azim", "span", None, None),
        P("azim", "span", None, None, None, None, None),
        P("azim", "span", None, None, None, None, None),
    )
    return jax.shard_map(
        shards, mesh=mesh, in_specs=placed, out_specs=P(None, None, "span", "azim"), check_vma=False
    )
```

```python
import functools
import math

import jax
import jax.numpy as jnp
from jax import lax
from jax.experimental import pallas as pl
from jax.experimental.pallas import tpu as pltpu
from jax.sharding import PartitionSpec as P

wavenumber = 0.9
coupling = 1.1
f32 = jnp.float32
bf16 = jnp.bfloat16

SEG = 8
SIN_POLY = (2.2214303951, -0.9131751650, 0.1098397679)


def split_two(value):
    high = value.astype(bf16)
    return high, (value - high.astype(f32)).astype(bf16)


def split_three(value):
    high = value.astype(bf16).astype(f32)
    rest = value - high
    middle = rest.astype(bf16).astype(f32)
    return high, middle, rest - middle


def dot_nt(left, right):
    return lax.dot_general(left, right, (((1,), (1,)), ((), ())), preferred_element_type=f32)


def segment_swap(value):
    rows = value.shape[1]
    row = lax.broadcasted_iota(jnp.int32, value.shape, 1)
    seg = lax.broadcasted_iota(jnp.int32, value.shape, 2) // SEG
    bit = 1
    while bit < rows:
        row_bit = (row // bit) % 2
        seg_bit = (seg // bit) % 2
        up = jnp.roll(jnp.roll(value, -bit, 1), SEG * bit, 2)
        down = jnp.roll(jnp.roll(value, bit, 1), -SEG * bit, 2)
        value = jnp.where(row_bit == seg_bit, value, jnp.where(row_bit == 0, up, down))
        bit *= 2
    return value


def pack(field_ref, pos_ref, nrm_ref, area_ref, out_ref, low_ref, high_ref):
    span_rows, width = area_ref.shape
    weight = area_ref[...] * (wavenumber / (2.0 * math.pi) / (4.0 * math.pi))
    field = field_ref[...].reshape(field_ref.shape[0] // span_rows, span_rows, width)
    parts = [field[q] * weight for q in range(field.shape[0])]
    parts += [pos_ref[i] for i in range(3)] + [nrm_ref[i] for i in range(3)]
    packed = segment_swap(jnp.stack(parts, 0))
    blocks = out_ref.shape[0]
    for q in range(len(parts)):
        out_ref[:, q, :] = packed[q]
        low_ref[:, q, :] = packed[q, : low_ref.shape[0]]
        high_ref[:, q, :] = packed[q, blocks - high_ref.shape[0] :]


def send_kernel(chosen_ref, count_ref, field_ref, pos_ref, nrm_ref, area_ref, v_hbm, *rest):
    out_ref, mid_ref, low_ref, high_ref, v_ref, table_ref, sems = rest
    chunks = sems.shape[0]
    peers = out_ref.shape[0] // chunks
    rank = v_ref.shape[3]
    cap = v_ref.shape[1]
    width = out_ref.shape[2]
    span_rows = table_ref.shape[0]

    def fetch(index):
        rows = pl.ds(index * peers, peers)
        return pltpu.make_async_copy(v_hbm.at[rows], v_ref.at[rows], sems.at[index])

    for index in range(chunks):
        fetch(index).start()
    pack(field_ref, pos_ref, nrm_ref, area_ref, mid_ref, low_ref, high_ref)

    half = field_ref.shape[0] // 2
    for row in range(span_rows):
        re, im = (field_ref[pl.ds(c * half + row, 8, stride=span_rows), :] for c in range(2))
        high, low = split_two(
            jnp.concatenate(
                [jnp.concatenate([re, -im], 1), jnp.concatenate([im, re], 1)], 0
            )
        )
        table_ref[row] = jnp.concatenate([high, low], 0)

    def one_chunk(index, carry):
        fetch(index).wait()
        for i in range(peers):
            peer = index * peers + i
            right = jnp.concatenate(
                [jnp.concatenate([v_ref[peer, k, 0], v_ref[peer, k, 1]], 1) for k in range(cap)], 0
            )
            high, low = split_two(right)
            rows = [table_ref[chosen_ref[k, peer]] for k in range(cap)]
            first = dot_nt(jnp.concatenate(rows, 0), high)
            second = dot_nt(jnp.concatenate([r[:16] for r in rows], 0), low)
            tile = []
            for k in range(cap):
                both = first[32 * k : 32 * k + 16] + (
                    first[32 * k + 16 : 32 * k + 32] + second[16 * k : 16 * k + 16]
                )
                both = jnp.where(k < count_ref[0, peer], both, 0.0)
                cols = slice(k * rank, (k + 1) * rank)
                tile += [both[:8, cols], both[8:, cols]]
            tile.append(jnp.zeros((8, width - 2 * rank * cap), f32))
            out_ref[peer] = jnp.concatenate(tile, 1)
        return carry

    lax.fori_loop(0, chunks, one_chunk, 0)


def receive_kernel(target_ref, me_ref, coef_ref, u_ref, *rest):
    outs, accs = rest[:-4], rest[-4:]
    span = len(outs)
    count, cap, rank, width = u_ref.shape[0], u_ref.shape[1], u_ref.shape[3], u_ref.shape[4]
    span_rows = outs[0].shape[1]
    used = 2 * rank * cap
    row_bits = span_rows.bit_length() - 1
    piece = accs[0].shape[0] // span
    peers = 16
    for acc_ref in accs:
        acc_ref[...] = jnp.zeros_like(acc_ref)
    me = me_ref[0]
    lane = lax.broadcasted_iota(jnp.int32, (peers * 8, width), 1)

    def one_chunk(index, carry):
        coef = coef_ref[pl.ds(index * peers, peers)].reshape(peers * 8, width)
        is_im = (lane // rank) % 2 == 1
        real_row = jnp.where(is_im, -coef, coef)
        imag_row = jnp.where(is_im, jnp.roll(coef, rank, 1), jnp.roll(coef, -rank, 1))
        zero = jnp.zeros_like(coef)
        rows = []
        for k in range(cap):
            here = lane // (2 * rank) == k
            rows += [jnp.where(here, real_row, zero), jnp.where(here, imag_row, zero)]
        for i in range(peers):
            peer = index * peers + i
            left = jnp.concatenate([r[8 * i : 8 * i + 8, :used] for r in rows], 0)
            left_high, left_low = split_two(left)
            high, low = split_two(u_ref[peer].reshape(used, width))
            one = jnp.dot(
                jnp.concatenate([left_high, left_low], 0), high, preferred_element_type=f32
            )
            two = jnp.dot(left_high, low, preferred_element_type=f32)
            many = left.shape[0]
            total = one[:many] + (one[many:] + two)
            for k in range(cap):
                w = target_ref[k, peer]
                place = (((w >> row_bits) - me) & (span - 1)) * piece + (w & (span_rows - 1))
                at = pl.ds(place, 16, stride=span_rows)
                acc_ref = accs[(2 * i + k) % 4]
                acc_ref[at, :] += total[16 * k : 16 * k + 16]
        return carry

    lax.fori_loop(0, count // peers, one_chunk, 0)
    for k in range(span):
        at = slice(k * piece, (k + 1) * piece)
        total = (accs[0][at, :] + accs[1][at, :]) + (accs[2][at, :] + accs[3][at, :])
        outs[k][...] = total.reshape(outs[k].shape)


def near_kernel(begin, count, skip, edge, *refs):
    scratch = refs[-7:]
    pos_ref, wide_ref, kern_ref, target_ref, source_ref, part_ref, acc_ref = scratch
    if edge:
        left_ref, mid_ref, right_ref, done_ref, field_ref, out_ref = refs[:-7]
    else:
        mid_ref, out_ref, token_ref = refs[:-7]
    blocks = mid_ref.shape[0]
    halo = blocks // 4
    window = 2 * halo + 1
    width = mid_ref.shape[2]
    turn = wavenumber / (2.0 * math.pi)

    def block_in(index):
        if index < halo:
            return left_ref.at[index]
        if index < halo + blocks:
            return mid_ref.at[index - halo]
        return right_ref.at[index - halo - blocks]

    origin = mid_ref[blocks // 2, 16:19, 0:1]
    row = lax.broadcasted_iota(jnp.int32, (8, width), 0)
    for b in range(0 if edge else halo, blocks + (2 if edge else 1) * halo):
        ref = block_in(b)
        pad = jnp.zeros((5, width), f32)
        pos_ref[b, 0:8, :] = jnp.concatenate([(ref[16:19, :] - origin) * turn, pad], 0)
        pos_ref[b, 8:16, :] = jnp.concatenate([ref[19:22, :] * wavenumber, pad], 0)
        re, im = ref[0:8, :], ref[8:16, :]
        rows = jnp.concatenate(
            [jnp.concatenate([re, -im], 1), jnp.concatenate([im, re], 1)], 0
        )
        high, low = split_two(rows)
        wide_ref[:, 2 * width * b : 2 * width * (b + 1)] = jnp.concatenate([high, low], 0).astype(f32)
    sources = window + 1
    zeros = jnp.zeros((width, 2 * width), f32)
    for part in (0, 2):
        kern_ref[(part + 1) * width : (part + 2) * width, : 2 * width] = zeros
        kern_ref[part * width : (part + 1) * width, 2 * width * (sources - 1) :] = zeros

    chunk = 16
    sub = lax.broadcasted_iota(jnp.int32, (chunk, width), 0)
    lane = lax.broadcasted_iota(jnp.int32, (chunk, width), 1)

    def evaluate(squared, num, at, offset):
        if offset == 0:
            self_pair = (sub + at) == lane
            squared = jnp.where(self_pair, 1.0, squared)
        inv = lax.rsqrt(squared)
        turns = squared * inv
        frac = turns - jnp.round(turns)
        z = frac * frac
        s1 = frac * (SIN_POLY[0] + z * (SIN_POLY[1] + z * SIN_POLY[2]))
        s1_sq = s1 * s1
        c1_sq = 2.0 - s1_sq
        s2 = s1 * (c1_sq * lax.rsqrt(c1_sq))
        c2 = c1_sq - s1_sq
        sine = s2 * c2
        cosine = 1.0 - s2 * (s2 + s2)
        if offset == 0:
            inv = jnp.where(self_pair, 0.0, inv)
        if offset == -halo:
            inv = jnp.where(lane % SEG >= sub % SEG, inv, 0.0)
        if offset == halo:
            inv = jnp.where(lane % SEG <= sub % SEG, inv, 0.0)
        slant = num * inv
        first = (slant * (turn / wavenumber)) * inv
        second = slant + coupling
        pc, ps = inv * cosine, inv * sine
        return first * pc + second * ps, first * ps - second * pc

    def pair_of(step):
        return jnp.where(step < count, step, step + skip) + begin

    def prepare(step, carry):
        tp = pair_of(step)
        center = pos_ref[2 * tp + halo, 0:8, 8 * SEG - 1 : 8 * SEG]

        def local_of(index):
            place = pos_ref[2 * tp + index, 0:8, :] - center
            return place, jnp.sum(place * place, axis=0, keepdims=True)

        for t in range(2):
            place, norm = local_of(halo + t)
            high, mid, low = split_three(
                jnp.where(row < 3, place, jnp.where(row == 3, 1.0, jnp.where(row == 4, norm, 0.0)))
            )
            rows = jnp.transpose(jnp.concatenate([high, high, mid, high, mid, low], 0))
            target_ref[step, t * width : (t + 1) * width, :] = rows.astype(bf16)
        for sb in range(sources):
            place, norm = local_of(sb)
            normal = pos_ref[2 * tp + sb, 8:16, :]
            along = jnp.sum(normal * place, axis=0, keepdims=True)
            wide = []
            for rows in (
                jnp.where(
                    row < 3, -2.0 * place, jnp.where(row == 3, norm, jnp.where(row == 4, 1.0, 0.0))
                ),
                jnp.where(row < 3, normal, jnp.where(row == 3, -along, 0.0)),
            ):
                high, mid, low = split_three(rows)
                wide.append(jnp.concatenate([high, mid, high, low, mid, high], 0))
            cols = slice(2 * width * sb, 2 * width * (sb + 1))
            source_ref[step, :, cols] = jnp.concatenate(wide, 1).astype(bf16)
        return carry

    batch = 2

    def sums(step, index):
        size = 2 * width * batch
        start = pl.multiple_of(pair_of(step) * (4 * width) + size * index, 2 * width)
        prod = dot_nt(
            kern_ref[:, size * index : size * (index + 1)], wide_ref[:, pl.ds(start, size)]
        )
        return prod[: 2 * width] + prod[2 * width :]

    def finish(step, slot):
        prod = part_ref[...] + sums(step, sources // batch - 1)
        for t in range(2):
            half = jnp.transpose(prod[t * width : (t + 1) * width])
            acc_ref[:, pl.ds(2 * slot + t, 1), :] = (half[:16] + half[16:])[:, None, :]

    pairs = 2 * count if edge else count
    spare = acc_ref.shape[1] // 2 - 1

    def slot_of(step):
        return pair_of(step) if edge else step

    def rows_of(sb):
        return (width if sb == sources - 1 else 0), (width if sb == 0 else 2 * width)

    def gram_of(step, sb):
        start, stop = rows_of(sb)
        return jnp.dot(
            target_ref[step, start:stop, :],
            source_ref[step, :, 2 * width * sb : 2 * width * (sb + 1)],
            preferred_element_type=f32,
        )

    def one_pair(step, carry):
        for sb in range(sources):
            start, stop = rows_of(sb)
            gram = gram_of(step, sb)
            done = sb - 1 if sb % batch == 1 % batch else -1
            if sb == 1:
                last = jnp.maximum(step - 1, 0)
                finish(last, jnp.where(step == 0, spare, slot_of(last)))
            elif sb > batch and done >= 0:
                index = done // batch - 1
                if index == 0:
                    part_ref[...] = sums(step, 0)
                else:
                    part_ref[...] += sums(step, index)
            for at in range(start, stop, chunk):
                t = at // width
                part = gram[at - start : at - start + chunk]
                kern = evaluate(part[:, :width], part[:, width:], at % width, sb - halo - t)
                for value, shift in zip(kern, (0, width)):
                    high, low = value, value - value.astype(bf16).astype(f32)
                    cols = slice(2 * width * sb + shift, 2 * width * sb + shift + width)
                    kern_ref[at : at + chunk, cols] = high
                    kern_ref[2 * width + at : 2 * width + at + chunk, cols] = low
        return carry

    part_ref[...] = jnp.zeros_like(part_ref)
    lax.fori_loop(0, pairs, prepare, 0, unroll=True)
    lax.fori_loop(0, pairs, one_pair, 0)
    finish(pairs - 1, slot_of(pairs - 1))
    if edge:
        acc_ref[:, 2 * count : 2 * (count + skip), :] = done_ref[...]
        swapped = segment_swap(acc_ref[:, :blocks, :])
        rhs_count = field_ref.shape[1]
        for c in range(2):
            for u in range(rhs_count):
                out_ref[c, u] = swapped[c * rhs_count + u] + 0.5 * field_ref[c, u]
    else:
        out_ref[...] = acc_ref[:, : 2 * pairs, :]
        token_ref[...] = jnp.zeros_like(token_ref)


def vmem(count=1):
    return [pl.BlockSpec(memory_space=pltpu.VMEM)] * count


def smem(count=1):
    return [pl.BlockSpec(memory_space=pltpu.SMEM)] * count


def cost(flops, size):
    return pl.CostEstimate(flops=flops, bytes_accessed=size, transcendentals=0)


def params(megabytes):
    return pltpu.CompilerParams(vmem_limit_bytes=megabytes * 1024 * 1024)


def run_send(chosen, counts, field, positions, normals, areas, v):
    peers, cap, _, rank, width = v.shape
    rhs, span_rows = field.shape[1:3]
    chunks = 4
    blocks = width // SEG
    halo = blocks // 4
    shapes = [(peers, 8, width), (blocks, 24, width), (halo, 24, width), (halo, 24, width)]
    return pl.pallas_call(
        send_kernel,
        in_specs=smem(2) + vmem(4) + [pl.BlockSpec(memory_space=pl.ANY)],
        out_specs=vmem(4),
        out_shape=[jax.ShapeDtypeStruct(s, f32) for s in shapes],
        scratch_shapes=[
            pltpu.VMEM(v.shape, f32),
            pltpu.VMEM((span_rows, 32, 2 * width), bf16),
            pltpu.SemaphoreType.DMA((chunks,)),
        ],
        cost_estimate=cost(3 * 10**9, 4 * v.size),
        compiler_params=params(58),
        name="send",
    )(chosen, counts, field.reshape(2 * rhs * span_rows, width), positions, normals, areas, v)


def run_receive(targets, me, coef, u, span, span_rows):
    width = u.shape[4]
    shape = (16, span_rows, width)
    return pl.pallas_call(
        receive_kernel,
        in_specs=smem(2) + vmem(2),
        out_specs=vmem(span),
        out_shape=[jax.ShapeDtypeStruct(shape, f32)] * span,
        scratch_shapes=[pltpu.VMEM((span * 16 * span_rows, width), f32)] * 4,
        cost_estimate=cost(3 * 10**9, 4 * u.size),
        compiler_params=params(12),
        name="receive",
    )(targets, me, coef, u)


def near_scratch(blocks, width, pairs, slots):
    halo = blocks // 4
    count = blocks + 2 * halo
    span = 2 * width * (2 * halo + 2)
    return [
        pltpu.VMEM((count, 16, width), f32),
        pltpu.VMEM((32, 2 * width * count), f32),
        pltpu.VMEM((4 * width, span), f32),
        pltpu.VMEM((pairs, 2 * width, 48), bf16),
        pltpu.VMEM((pairs, 48, span), bf16),
        pltpu.VMEM((2 * width, 32), f32),
        pltpu.VMEM((16, 2 * slots + 2, width), f32),
    ]


def run_near_inner(mid):
    blocks, _, width = mid.shape
    halo = blocks // 4
    count = blocks - 2 * halo
    return pl.pallas_call(
        functools.partial(near_kernel, halo // 2, count // 2, 0, False),
        in_specs=vmem(1),
        out_specs=vmem(2),
        out_shape=[
            jax.ShapeDtypeStruct((16, count, width), f32),
            jax.ShapeDtypeStruct((8, width), f32),
        ],
        scratch_shapes=near_scratch(blocks, width, count // 2, count // 2),
        compiler_params=params(20),
        cost_estimate=cost(10**10, 10**6),
        name="near_inner",
    )(mid)


def run_near_edge(left, mid, right, done, field):
    blocks, _, width = mid.shape
    halo = left.shape[0]
    return pl.pallas_call(
        functools.partial(near_kernel, 0, halo // 2, blocks // 2 - halo, True),
        in_specs=vmem(5),
        out_specs=vmem()[0],
        out_shape=jax.ShapeDtypeStruct(field.shape, f32),
        scratch_shapes=near_scratch(blocks, width, halo, blocks // 2),
        compiler_params=params(20),
        cost_estimate=cost(10**10, 10**6),
        name="near_edge",
    )(left, mid, right, done, field)


def shards(
    field, positions, normals, areas, col_cluster, block_count, row_cluster, v_factors, u_factors
):
    azim = lax.axis_size("azim")
    span = lax.axis_size("span")
    span_rows = field.shape[2]
    hold = lax.optimization_barrier
    outgoing, mid, low, high = run_send(
        col_cluster[0, 0].T,
        block_count[0],
        field,
        positions,
        normals,
        areas,
        v_factors.reshape(v_factors.shape[2:]),
    )
    incoming = lax.all_to_all(outgoing, "azim", split_axis=0, concat_axis=0, tiled=True)
    forward = [(i, (i + 1) % azim) for i in range(azim)]
    backward = [(b, a) for a, b in forward]
    left = lax.ppermute(high, "azim", forward)
    right = lax.ppermute(low, "azim", backward)
    inner, token = run_near_inner(mid)
    incoming, _ = hold((incoming, token))
    me = lax.axis_index("span").astype(jnp.int32).reshape(1)
    pieces = run_receive(
        row_cluster[0, 0].T, me, incoming, u_factors.reshape(u_factors.shape[2:]), span, span_rows
    )
    mid, *pieces = hold((mid, *pieces))
    total = pieces[0]
    others = []
    for k in range(1, span):
        ring = [(i, (i + k) % span) for i in range(span)]
        others.append(lax.ppermute(pieces[k], "span", ring))
    near = run_near_edge(left, mid, right, inner, field)
    for other in others:
        total = total + other
    return near + total.reshape(near.shape)


def solution(mesh):
    placed = (
        P(None, None, "span", "azim"),
        P(None, "span", "azim"),
        P(None, "span", "azim"),
        P("span", "azim"),
        P("azim", "span", None, None),
        P("azim", "span", None),
        P("azim", "span", None, None),
        P("azim", "span", None, None, None, None, None),
        P("azim", "span", None, None, None, None, None),
    )
    return jax.shard_map(
        shards, mesh=mesh, in_specs=placed, out_specs=P(None, None, "span", "azim"), check_vma=False
    )
```

```python
import functools
import math

import jax
import jax.numpy as jnp
from jax import lax
from jax.experimental import pallas as pl
from jax.experimental.pallas import tpu as pltpu
from jax.sharding import PartitionSpec as P

wavenumber = 0.9
coupling = 1.1
f32 = jnp.float32
bf16 = jnp.bfloat16

SEG = 8
SIN_POLY = (2.2214303951, -0.9131751650, 0.1098397679)


def split_two(value):
    high = value.astype(bf16)
    return high, (value - high.astype(f32)).astype(bf16)


def split_three(value):
    high = value.astype(bf16).astype(f32)
    rest = value - high
    middle = rest.astype(bf16).astype(f32)
    return high, middle, rest - middle


def dot_nt(left, right):
    return lax.dot_general(left, right, (((1,), (1,)), ((), ())), preferred_element_type=f32)


def segment_swap(value):
    rows = value.shape[1]
    row = lax.broadcasted_iota(jnp.int32, value.shape, 1)
    seg = lax.broadcasted_iota(jnp.int32, value.shape, 2) // SEG
    bit = 1
    while bit < rows:
        row_bit = (row // bit) % 2
        seg_bit = (seg // bit) % 2
        up = jnp.roll(jnp.roll(value, -bit, 1), SEG * bit, 2)
        down = jnp.roll(jnp.roll(value, bit, 1), -SEG * bit, 2)
        value = jnp.where(row_bit == seg_bit, value, jnp.where(row_bit == 0, up, down))
        bit *= 2
    return value


def pack(field_ref, pos_ref, nrm_ref, area_ref, out_ref, low_ref, high_ref):
    span_rows, width = area_ref.shape
    weight = area_ref[...] * (wavenumber / (2.0 * math.pi) / (4.0 * math.pi))
    field = field_ref[...].reshape(field_ref.shape[0] // span_rows, span_rows, width)
    parts = [field[q] * weight for q in range(field.shape[0])]
    parts += [pos_ref[i] for i in range(3)] + [nrm_ref[i] for i in range(3)]
    packed = segment_swap(jnp.stack(parts, 0))
    blocks = out_ref.shape[0]
    for q in range(len(parts)):
        out_ref[:, q, :] = packed[q]
        low_ref[:, q, :] = packed[q, : low_ref.shape[0]]
        high_ref[:, q, :] = packed[q, blocks - high_ref.shape[0] :]


def send_kernel(chosen_ref, count_ref, field_ref, pos_ref, nrm_ref, area_ref, v_hbm, *rest):
    out_ref, mid_ref, low_ref, high_ref, v_ref, table_ref, sems = rest
    chunks = sems.shape[0]
    peers = out_ref.shape[0] // chunks
    rank = v_ref.shape[3]
    cap = v_ref.shape[1]
    width = out_ref.shape[2]
    span_rows = table_ref.shape[0]

    def fetch(index):
        rows = pl.ds(index * peers, peers)
        return pltpu.make_async_copy(v_hbm.at[rows], v_ref.at[rows], sems.at[index])

    for index in range(chunks):
        fetch(index).start()
    pack(field_ref, pos_ref, nrm_ref, area_ref, mid_ref, low_ref, high_ref)

    half = field_ref.shape[0] // 2
    for row in range(span_rows):
        re, im = (field_ref[pl.ds(c * half + row, 8, stride=span_rows), :] for c in range(2))
        high, low = split_two(
            jnp.concatenate(
                [jnp.concatenate([re, -im], 1), jnp.concatenate([im, re], 1)], 0
            )
        )
        table_ref[row] = jnp.concatenate([high, low], 0)

    def one_chunk(index, carry):
        fetch(index).wait()
        for i in range(peers):
            peer = index * peers + i
            right = jnp.concatenate(
                [jnp.concatenate([v_ref[peer, k, 0], v_ref[peer, k, 1]], 1) for k in range(cap)], 0
            )
            high, low = split_two(right)
            rows = [table_ref[chosen_ref[k, peer]] for k in range(cap)]
            first = dot_nt(jnp.concatenate(rows, 0), high)
            second = dot_nt(jnp.concatenate([r[:16] for r in rows], 0), low)
            tile = []
            for k in range(cap):
                both = first[32 * k : 32 * k + 16] + (
                    first[32 * k + 16 : 32 * k + 32] + second[16 * k : 16 * k + 16]
                )
                both = jnp.where(k < count_ref[0, peer], both, 0.0)
                cols = slice(k * rank, (k + 1) * rank)
                tile += [both[:8, cols], both[8:, cols]]
            tile.append(jnp.zeros((8, width - 2 * rank * cap), f32))
            out_ref[peer] = jnp.concatenate(tile, 1)
        return carry

    lax.fori_loop(0, chunks, one_chunk, 0)


def receive_kernel(target_ref, me_ref, coef_ref, u_ref, *rest):
    outs, accs = rest[:-4], rest[-4:]
    span = len(outs)
    count, cap, rank, width = u_ref.shape[0], u_ref.shape[1], u_ref.shape[3], u_ref.shape[4]
    span_rows = outs[0].shape[1]
    used = 2 * rank * cap
    row_bits = span_rows.bit_length() - 1
    piece = accs[0].shape[0] // span
    peers = 32
    for acc_ref in accs:
        acc_ref[...] = jnp.zeros_like(acc_ref)
    me = me_ref[0]
    lane = lax.broadcasted_iota(jnp.int32, (peers * 8, width), 1)

    def one_chunk(index, carry):
        coef = coef_ref[pl.ds(index * peers, peers)].reshape(peers * 8, width)
        is_im = (lane // rank) % 2 == 1
        real_row = jnp.where(is_im, -coef, coef)
        imag_row = jnp.where(is_im, jnp.roll(coef, rank, 1), jnp.roll(coef, -rank, 1))
        zero = jnp.zeros_like(coef)
        rows = []
        for k in range(cap):
            here = lane // (2 * rank) == k
            rows += [jnp.where(here, real_row, zero), jnp.where(here, imag_row, zero)]
        for i in range(peers):
            peer = index * peers + i
            left = jnp.concatenate([r[8 * i : 8 * i + 8, :used] for r in rows], 0)
            left_high, left_low = split_two(left)
            high, low = split_two(u_ref[peer].reshape(used, width))
            one = jnp.dot(
                jnp.concatenate([left_high, left_low], 0), high, preferred_element_type=f32
            )
            two = jnp.dot(left_high, low, preferred_element_type=f32)
            many = left.shape[0]
            total = one[:many] + (one[many:] + two)
            for k in range(cap):
                w = target_ref[k, peer]
                place = (((w >> row_bits) - me) & (span - 1)) * piece + (w & (span_rows - 1))
                at = pl.ds(place, 16, stride=span_rows)
                acc_ref = accs[(2 * i + k) % 4]
                acc_ref[at, :] += total[16 * k : 16 * k + 16]
        return carry

    lax.fori_loop(0, count // peers, one_chunk, 0)
    for k in range(span):
        at = slice(k * piece, (k + 1) * piece)
        total = (accs[0][at, :] + accs[1][at, :]) + (accs[2][at, :] + accs[3][at, :])
        outs[k][...] = total.reshape(outs[k].shape)


def near_kernel(begin, count, skip, edge, *refs):
    scratch = refs[-7:]
    pos_ref, wide_ref, kern_ref, target_ref, source_ref, part_ref, acc_ref = scratch
    if edge:
        left_ref, mid_ref, right_ref, done_ref, field_ref, out_ref = refs[:-7]
    else:
        mid_ref, out_ref, token_ref = refs[:-7]
    blocks = mid_ref.shape[0]
    halo = blocks // 4
    window = 2 * halo + 1
    width = mid_ref.shape[2]
    turn = wavenumber / (2.0 * math.pi)

    def block_in(index):
        if index < halo:
            return left_ref.at[index]
        if index < halo + blocks:
            return mid_ref.at[index - halo]
        return right_ref.at[index - halo - blocks]

    origin = mid_ref[blocks // 2, 16:19, 0:1]
    row = lax.broadcasted_iota(jnp.int32, (8, width), 0)
    for b in range(0 if edge else halo, blocks + (2 if edge else 1) * halo):
        ref = block_in(b)
        pad = jnp.zeros((5, width), f32)
        pos_ref[b, 0:8, :] = jnp.concatenate([(ref[16:19, :] - origin) * turn, pad], 0)
        pos_ref[b, 8:16, :] = jnp.concatenate([ref[19:22, :] * wavenumber, pad], 0)
        re, im = ref[0:8, :], ref[8:16, :]
        rows = jnp.concatenate(
            [jnp.concatenate([re, -im], 1), jnp.concatenate([im, re], 1)], 0
        )
        high, low = split_two(rows)
        wide_ref[:, 2 * width * b : 2 * width * (b + 1)] = jnp.concatenate([high, low], 0).astype(f32)
    sources = window + 1
    zeros = jnp.zeros((width, 2 * width), f32)
    for part in (0, 2):
        kern_ref[(part + 1) * width : (part + 2) * width, : 2 * width] = zeros
        kern_ref[part * width : (part + 1) * width, 2 * width * (sources - 1) :] = zeros

    chunk = 32
    sub = lax.broadcasted_iota(jnp.int32, (chunk, width), 0)
    lane = lax.broadcasted_iota(jnp.int32, (chunk, width), 1)

    def evaluate(squared, num, at, offset):
        if offset == 0:
            self_pair = (sub + at) == lane
            squared = jnp.where(self_pair, 1.0, squared)
        inv = lax.rsqrt(squared)
        turns = squared * inv
        frac = turns - jnp.round(turns)
        z = frac * frac
        s1 = frac * (SIN_POLY[0] + z * (SIN_POLY[1] + z * SIN_POLY[2]))
        s1_sq = s1 * s1
        c1_sq = 2.0 - s1_sq
        s2 = s1 * (c1_sq * lax.rsqrt(c1_sq))
        c2 = c1_sq - s1_sq
        sine = s2 * c2
        cosine = 1.0 - s2 * (s2 + s2)
        if offset == 0:
            inv = jnp.where(self_pair, 0.0, inv)
        if offset == -halo:
            inv = jnp.where(lane % SEG >= sub % SEG, inv, 0.0)
        if offset == halo:
            inv = jnp.where(lane % SEG <= sub % SEG, inv, 0.0)
        slant = num * inv
        first = (slant * (turn / wavenumber)) * inv
        second = slant + coupling
        pc, ps = inv * cosine, inv * sine
        return first * pc + second * ps, first * ps - second * pc

    def pair_of(step):
        return jnp.where(step < count, step, step + skip) + begin

    def prepare(step, carry):
        tp = pair_of(step)
        center = pos_ref[2 * tp + halo, 0:8, 8 * SEG - 1 : 8 * SEG]

        def local_of(index):
            place = pos_ref[2 * tp + index, 0:8, :] - center
            return place, jnp.sum(place * place, axis=0, keepdims=True)

        for t in range(2):
            place, norm = local_of(halo + t)
            high, mid, low = split_three(
                jnp.where(row < 3, place, jnp.where(row == 3, 1.0, jnp.where(row == 4, norm, 0.0)))
            )
            rows = jnp.transpose(jnp.concatenate([high, high, mid, high, mid, low], 0))
            target_ref[step, t * width : (t + 1) * width, :] = rows.astype(bf16)
        for sb in range(sources):
            place, norm = local_of(sb)
            normal = pos_ref[2 * tp + sb, 8:16, :]
            along = jnp.sum(normal * place, axis=0, keepdims=True)
            wide = []
            for rows in (
                jnp.where(
                    row < 3, -2.0 * place, jnp.where(row == 3, norm, jnp.where(row == 4, 1.0, 0.0))
                ),
                jnp.where(row < 3, normal, jnp.where(row == 3, -along, 0.0)),
            ):
                high, mid, low = split_three(rows)
                wide.append(jnp.concatenate([high, mid, high, low, mid, high], 0))
            cols = slice(2 * width * sb, 2 * width * (sb + 1))
            source_ref[step, :, cols] = jnp.concatenate(wide, 1).astype(bf16)
        return carry

    batch = 2

    def sums(step, index):
        size = 2 * width * batch
        start = pl.multiple_of(pair_of(step) * (4 * width) + size * index, 2 * width)
        prod = dot_nt(
            kern_ref[:, size * index : size * (index + 1)], wide_ref[:, pl.ds(start, size)]
        )
        return prod[: 2 * width] + prod[2 * width :]

    def finish(step, slot):
        prod = part_ref[...] + sums(step, sources // batch - 1)
        for t in range(2):
            half = jnp.transpose(prod[t * width : (t + 1) * width])
            acc_ref[:, pl.ds(2 * slot + t, 1), :] = (half[:16] + half[16:])[:, None, :]

    pairs = 2 * count if edge else count
    spare = acc_ref.shape[1] // 2 - 1

    def slot_of(step):
        return pair_of(step) if edge else step

    def rows_of(sb):
        return (width if sb == sources - 1 else 0), (width if sb == 0 else 2 * width)

    def gram_of(step, sb):
        start, stop = rows_of(sb)
        return jnp.dot(
            target_ref[step, start:stop, :],
            source_ref[step, :, 2 * width * sb : 2 * width * (sb + 1)],
            preferred_element_type=f32,
        )

    def one_pair(step, carry):
        for sb in range(sources):
            start, stop = rows_of(sb)
            gram = gram_of(step, sb)
            done = sb - 1 if sb % batch == 1 % batch else -1
            if sb == 1:
                last = jnp.maximum(step - 1, 0)
                finish(last, jnp.where(step == 0, spare, slot_of(last)))
            elif sb > batch and done >= 0:
                index = done // batch - 1
                if index == 0:
                    part_ref[...] = sums(step, 0)
                else:
                    part_ref[...] += sums(step, index)
            for at in range(start, stop, chunk):
                t = at // width
                part = gram[at - start : at - start + chunk]
                kern = evaluate(part[:, :width], part[:, width:], at % width, sb - halo - t)
                for value, shift in zip(kern, (0, width)):
                    high, low = value, value - value.astype(bf16).astype(f32)
                    cols = slice(2 * width * sb + shift, 2 * width * sb + shift + width)
                    kern_ref[at : at + chunk, cols] = high
                    kern_ref[2 * width + at : 2 * width + at + chunk, cols] = low
        return carry

    part_ref[...] = jnp.zeros_like(part_ref)
    lax.fori_loop(0, pairs, prepare, 0, unroll=True)
    lax.fori_loop(0, pairs, one_pair, 0)
    finish(pairs - 1, slot_of(pairs - 1))
    if edge:
        acc_ref[:, 2 * count : 2 * (count + skip), :] = done_ref[...]
        swapped = segment_swap(acc_ref[:, :blocks, :])
        rhs_count = field_ref.shape[1]
        for c in range(2):
            for u in range(rhs_count):
                out_ref[c, u] = swapped[c * rhs_count + u] + 0.5 * field_ref[c, u]
    else:
        out_ref[...] = acc_ref[:, : 2 * pairs, :]
        token_ref[...] = jnp.zeros_like(token_ref)


def vmem(count=1):
    return [pl.BlockSpec(memory_space=pltpu.VMEM)] * count


def smem(count=1):
    return [pl.BlockSpec(memory_space=pltpu.SMEM)] * count


def cost(flops, size):
    return pl.CostEstimate(flops=flops, bytes_accessed=size, transcendentals=0)


def params(megabytes):
    return pltpu.CompilerParams(vmem_limit_bytes=megabytes * 1024 * 1024)


def run_send(chosen, counts, field, positions, normals, areas, v):
    peers, cap, _, rank, width = v.shape
    rhs, span_rows = field.shape[1:3]
    chunks = 4
    blocks = width // SEG
    halo = blocks // 4
    shapes = [(peers, 8, width), (blocks, 24, width), (halo, 24, width), (halo, 24, width)]
    return pl.pallas_call(
        send_kernel,
        in_specs=smem(2) + vmem(4) + [pl.BlockSpec(memory_space=pl.ANY)],
        out_specs=vmem(4),
        out_shape=[jax.ShapeDtypeStruct(s, f32) for s in shapes],
        scratch_shapes=[
            pltpu.VMEM(v.shape, f32),
            pltpu.VMEM((span_rows, 32, 2 * width), bf16),
            pltpu.SemaphoreType.DMA((chunks,)),
        ],
        cost_estimate=cost(3 * 10**9, 4 * v.size),
        compiler_params=params(58),
        name="send",
    )(chosen, counts, field.reshape(2 * rhs * span_rows, width), positions, normals, areas, v)


def run_receive(targets, me, coef, u, span, span_rows):
    width = u.shape[4]
    shape = (16, span_rows, width)
    return pl.pallas_call(
        receive_kernel,
        in_specs=smem(2) + vmem(2),
        out_specs=vmem(span),
        out_shape=[jax.ShapeDtypeStruct(shape, f32)] * span,
        scratch_shapes=[pltpu.VMEM((span * 16 * span_rows, width), f32)] * 4,
        cost_estimate=cost(3 * 10**9, 4 * u.size),
        compiler_params=params(12),
        name="receive",
    )(targets, me, coef, u)


def near_scratch(blocks, width, pairs, slots):
    halo = blocks // 4
    count = blocks + 2 * halo
    span = 2 * width * (2 * halo + 2)
    return [
        pltpu.VMEM((count, 16, width), f32),
        pltpu.VMEM((32, 2 * width * count), f32),
        pltpu.VMEM((4 * width, span), f32),
        pltpu.VMEM((pairs, 2 * width, 48), bf16),
        pltpu.VMEM((pairs, 48, span), bf16),
        pltpu.VMEM((2 * width, 32), f32),
        pltpu.VMEM((16, 2 * slots + 2, width), f32),
    ]


def run_near_inner(mid):
    blocks, _, width = mid.shape
    halo = blocks // 4
    count = blocks - 2 * halo
    return pl.pallas_call(
        functools.partial(near_kernel, halo // 2, count // 2, 0, False),
        in_specs=vmem(1),
        out_specs=vmem(2),
        out_shape=[
            jax.ShapeDtypeStruct((16, count, width), f32),
            jax.ShapeDtypeStruct((8, width), f32),
        ],
        scratch_shapes=near_scratch(blocks, width, count // 2, count // 2),
        compiler_params=params(20),
        cost_estimate=cost(10**10, 10**6),
        name="near_inner",
    )(mid)


def run_near_edge(left, mid, right, done, field):
    blocks, _, width = mid.shape
    halo = left.shape[0]
    return pl.pallas_call(
        functools.partial(near_kernel, 0, halo // 2, blocks // 2 - halo, True),
        in_specs=vmem(5),
        out_specs=vmem()[0],
        out_shape=jax.ShapeDtypeStruct(field.shape, f32),
        scratch_shapes=near_scratch(blocks, width, halo, blocks // 2),
        compiler_params=params(20),
        cost_estimate=cost(10**10, 10**6),
        name="near_edge",
    )(left, mid, right, done, field)


def shards(
    field, positions, normals, areas, col_cluster, block_count, row_cluster, v_factors, u_factors
):
    azim = lax.axis_size("azim")
    span = lax.axis_size("span")
    span_rows = field.shape[2]
    hold = lax.optimization_barrier
    outgoing, mid, low, high = run_send(
        col_cluster[0, 0].T,
        block_count[0],
        field,
        positions,
        normals,
        areas,
        v_factors.reshape(v_factors.shape[2:]),
    )
    incoming = lax.all_to_all(outgoing, "azim", split_axis=0, concat_axis=0, tiled=True)
    forward = [(i, (i + 1) % azim) for i in range(azim)]
    backward = [(b, a) for a, b in forward]
    left = lax.ppermute(high, "azim", forward)
    right = lax.ppermute(low, "azim", backward)
    inner, token = run_near_inner(mid)
    incoming, _ = hold((incoming, token))
    me = lax.axis_index("span").astype(jnp.int32).reshape(1)
    pieces = run_receive(
        row_cluster[0, 0].T, me, incoming, u_factors.reshape(u_factors.shape[2:]), span, span_rows
    )
    mid, *pieces = hold((mid, *pieces))
    total = pieces[0]
    others = []
    for k in range(1, span):
        ring = [(i, (i + k) % span) for i in range(span)]
        others.append(lax.ppermute(pieces[k], "span", ring))
    near = run_near_edge(left, mid, right, inner, field)
    for other in others:
        total = total + other
    return near + total.reshape(near.shape)


def solution(mesh):
    placed = (
        P(None, None, "span", "azim"),
        P(None, "span", "azim"),
        P(None, "span", "azim"),
        P("span", "azim"),
        P("azim", "span", None, None),
        P("azim", "span", None),
        P("azim", "span", None, None),
        P("azim", "span", None, None, None, None, None),
        P("azim", "span", None, None, None, None, None),
    )
    return jax.shard_map(
        shards, mesh=mesh, in_specs=placed, out_specs=P(None, None, "span", "azim"), check_vma=False
    )
```
